256 devices in a mesh: seq: 64 (over y, z, core), ch: 4 (over x).
Axes of the slice: x: 4, y: 4, z: 8, core: 2. Of those that a mesh axis runs over, the one named last changes fastest.
Arguments:
- stream: bfloat16 [8192, 8192], P('seq', 'ch'), may hold values from -3000 to 3000
- norm_gain: float32 [8192], P('ch'), may hold values from 0.5 to 1.5
- gate_act: bfloat16 [8192, 8192], P('seq', 'ch'), may hold values from -6 to 6
- decay_rate: float32 [8192, 16], P('ch'), may hold values from 0 to 1, as said below
- residue: float32 [8192, 16], P('ch'), may hold values from -1.5 to 1.5
- skip_gain: float32 [8192], P('ch'), may hold values from 0.5 to 1.5
Outputs:
- gated_output: bfloat16 [8192, 8192], P('seq', 'ch')
The draws below stay inside these ranges and needn't reach their ends.
Inputs may be any that keep to these rules, and one draw needn't show every extreme that they name: `decay_rate`: every rate is positive.
All inputs are finite; a program needn't handle non-finite values.
Results may differ from the reference program's by a relative error of at most 0.012.
Values may be sent and summed in bfloat16 or wider, within the bound.
A program may use at most 128 MiB of HBM per device.

```python
import math
import jax
import jax.numpy as jnp
from jax import lax

D = 8192
MODES = 16
TOKENS = 8192


def draw_stream(key, part):
    key = jax.random.fold_in(key, 11)
    key_noise, key_jitter = jax.random.split(key, 2)
    position = jnp.arange(D, dtype=jnp.float32) / D
    jitter = jnp.exp(0.35 * jax.random.uniform(key_jitter, (D,), jnp.float32, -1.0, 1.0))
    noise_draw = jnp.clip(jax.random.normal(key_noise, (TOKENS, D), jnp.float32), -4.0, 4.0)
    values = noise_draw * jnp.exp(math.log(10.0) * position) * jitter
    return values.astype(jnp.bfloat16)


def draw_decay_rate(key, part):
    key = jax.random.fold_in(key, 23)
    key_wide = jax.random.fold_in(key, 1)
    low_end = math.log(0.5 / TOKENS)
    high_end = math.log(1.0 / 30.0)
    wide_rates = jnp.exp(low_end + (high_end - low_end) * jax.random.uniform(key_wide, (D, MODES), jnp.float32))
    rates = wide_rates
    return rates.astype(jnp.float32)


def block_levels(own_key, extent, pieces, low, high):
    loudness, own = 1.0, jax.random.fold_in(own_key, 6)
    for dim, shards_of in pieces:
        draws = jnp.exp(jax.random.uniform(jax.random.fold_in(own, dim), (shards_of,), jnp.float32, low / len(pieces), high / len(pieces)))
        loudness = loudness * jnp.repeat(draws, extent[dim] // shards_of).reshape([-1 if axis == dim else 1 for axis in range(len(extent))])
    return loudness


def scatter_about(rng, shape, scale, limit, shards=(), kind=jnp.bfloat16):
    result = jax.random.normal(rng, shape, jnp.float32) * scale
    if len(shards) > 0:
        result = block_levels(rng, shape, shards, -0.22, 0.18) * result
    return jnp.clip(result, min=-limit, max=limit).astype(kind)


def setup_inputs(seed: int = 0) -> dict:
    keys = jax.random.split(jax.random.key(seed), 7)
    return {
        "stream": draw_stream(jax.random.fold_in(keys[6], 71), 0),
        "norm_gain": jnp.clip(1.0 + 0.1 * jax.random.normal(keys[1], (D,), jnp.float32), 0.5, 1.5),
        "gate_act": scatter_about(keys[2], (TOKENS, D), 1.0, 6.0, ((0, 64), (1, 4))),
        "decay_rate": draw_decay_rate(jax.random.fold_in(keys[6], 71), 0),
        "residue": scatter_about(keys[4], (D, MODES), MODES ** -0.5, 1.5, ((0, 4),), jnp.float32),
        "skip_gain": jnp.clip(0.5 + 1.0 * jax.random.uniform(keys[5], (D,), jnp.float32) ** block_levels(keys[5], (D,), ((0, 4),), -0.2, 0.2), 0.5, 1.5),
    }


eps_norm = 1e-06

def modal_sum(frequency, rate, weight, seq_length, padded):
    fraction = (frequency % padded).astype(jnp.float32) / padded
    half_sin = jnp.sin(math.pi * fraction)
    full_sin = jnp.sin(2.0 * math.pi * fraction)
    parity = (1 - 2 * (frequency % 2)).astype(jnp.float32)
    shape_all = tuple(frequency.shape[:-1]) + (rate.shape[0],)
    real_sum = jnp.zeros(shape_all, jnp.float32)
    imag_sum = jnp.zeros(shape_all, jnp.float32)
    for mode_idx in range(rate.shape[1]):
        rate_now = rate[:, mode_idx]
        factor = jnp.exp(-rate_now)
        shortfall = -jnp.expm1(-rate_now)
        remnant = jnp.exp(-rate_now * seq_length)
        scaled = weight[:, mode_idx] * jnp.sqrt(-jnp.expm1(-2.0 * rate_now))
        real_den = shortfall + 2.0 * factor * half_sin * half_sin
        imag_den = factor * full_sin
        numerator = scaled * (1.0 - remnant * parity)
        modulus = real_den * real_den + imag_den * imag_den
        real_sum = real_sum + numerator * real_den / modulus
        imag_sum = imag_sum - numerator * imag_den / modulus
    return (real_sum, imag_sum)

def reference(stream, norm_gain, gate_act, decay_rate, residue, skip_gain):
    values = stream.astype(jnp.float32)
    squares = lax.optimization_barrier(jnp.sum(values * values, axis=1))
    normed = (values * lax.rsqrt(squares / D + eps_norm)[:, None] * norm_gain).astype(jnp.bfloat16)
    padded = 2 * TOKENS
    block_width = math.gcd(D, 256)
    block_count = D // block_width
    blocks = normed.reshape(TOKENS, block_count, block_width).transpose(1, 0, 2)
    rates = decay_rate.reshape(block_count, block_width, MODES)
    weights = residue.reshape(block_count, block_width, MODES)
    frequency = jnp.arange(padded, dtype=jnp.int32)[:, None]

    def one_block(inputs):
        piece, rate_block, weight_block = inputs
        spectrum = jnp.fft.fft(piece.astype(jnp.float32), n=padded, axis=0)
        filt_real, filt_imag = modal_sum(frequency, rate_block, weight_block, TOKENS, padded)
        product = spectrum * lax.complex(filt_real, filt_imag)
        return jnp.real(jnp.fft.ifft(product, axis=0))[:TOKENS].astype(jnp.float32)
    conv = lax.map(one_block, (blocks, rates, weights))
    conv = conv.transpose(1, 0, 2).reshape(TOKENS, D)
    summed = conv + skip_gain * normed.astype(jnp.float32)
    return (summed * gate_act.astype(jnp.float32)).astype(jnp.bfloat16)
```

```python
import functools
import math

import jax
import jax.numpy as jnp
import numpy as np
from jax import lax
from jax.experimental import pallas as pl
from jax.experimental.pallas import tpu as pltpu
from jax.sharding import PartitionSpec as P

MESH = pl.DeviceIdType.MESH
EPS = 1e-06
LANES = 128
WIRE = jnp.bfloat16
F32 = jnp.float32
BF16 = jnp.bfloat16


def half_tables(length):
    k = np.arange(length)[:, None] + 0.5
    t = np.arange(length)[None, :]
    angle = np.pi * k * t / length
    forward = np.concatenate([np.cos(angle), -np.sin(angle)], axis=0)
    inverse = np.concatenate([np.cos(angle.T), -np.sin(angle.T)], axis=1) / length

    def split(table):
        high = table.astype(BF16)
        low = (table - high.astype(np.float64)).astype(BF16)
        return np.concatenate([high, low], axis=1)

    return split(forward), split(inverse)


def one_minus_exp_neg(z):
    series = jnp.ones_like(z)
    for n in range(10, 1, -1):
        series = 1.0 - z * series * (1.0 / n)
    return jnp.where(z < 0.5, z * series, 1.0 - jnp.exp(-z))


def total_of(items):
    items = list(items)
    while len(items) > 1:
        items = [a + b for a, b in zip(items[::2], items[1::2])] + ([items[-1]] if len(items) % 2 else [])
    return items[0]


def kernel(nx, ny, nj, modes, width,
           x_hbm, rate_hbm, res_hbm, gain_hbm, skip_hbm, gate_hbm, fwd_hbm, inv_hbm, out_ref,
           x_v, gate_v, rate_v, res_v, gain_v, skip_v, fwd_v, inv_v,
           sqacc_v, sq_v, scol_v, pow_v, taps_v, xn_v, conv_v, srow_v,
           st_out, st_in, tot_v, pre_v, ca_out, ca_in,
           in_sem, x_sem, sq_send, sq_recv, st_send, st_recv, tot_send, tot_recv, ca_send, ca_recv):
    tokens, chans = x_v.shape
    blocks = chans // LANES
    mx = lax.axis_index("ch")
    seq = lax.axis_index("seq")
    my = seq // nj
    mj = lax.rem(seq, nj)

    def group_peer(k):
        return {"seq": my * nj + k}

    def spread(i):
        half = nj // 2
        return half + jnp.where(lax.rem(i, 2) == 1, (i + 1) // 2, -(i // 2))

    barrier = pltpu.get_barrier_semaphore()
    for d in range(1, nx):
        pl.semaphore_signal(barrier, inc=1, device_id={"ch": lax.rem(mx + d, nx)}, device_id_type=MESH)
    for d in range(1, ny):
        pl.semaphore_signal(barrier, inc=1, device_id={"seq": lax.rem(seq + d * nj, ny * nj)}, device_id_type=MESH)
    for d in range(1, nj):
        pl.semaphore_signal(barrier, inc=1, device_id=group_peer(lax.rem(mj + d, nj)), device_id_type=MESH)

    parts = x_sem.shape[0]
    rows_part = tokens // parts
    for p in range(parts):
        rows = pl.ds(p * rows_part, rows_part)
        pltpu.make_async_copy(x_hbm.at[rows], x_v.at[rows], x_sem.at[p]).start()
    staged = [(rate_hbm, rate_v), (res_hbm, res_v), (gain_hbm, gain_v), (skip_hbm, skip_v),
              (fwd_hbm, fwd_v), (inv_hbm, inv_v), (gate_hbm, gate_v)]
    staged = [pltpu.make_async_copy(a, b, in_sem.at[n]) for n, (a, b) in enumerate(staged)]
    for copy in staged:
        copy.start()

    tiles_part = rows_part // 16
    for p in range(parts):
        rows = pl.ds(p * rows_part, rows_part)
        pltpu.make_async_copy(x_hbm.at[rows], x_v.at[rows], x_sem.at[p]).wait()

        def square_rows(i, carry):
            part = pl.ds(pl.multiple_of(p * rows_part + i * 16, 16), 16)
            pieces = []
            for b in range(blocks):
                v = x_v[part, b * LANES:(b + 1) * LANES].astype(F32)
                pieces.append(v * v)
            sqacc_v[part, :] = total_of(pieces)
            return carry

        lax.fori_loop(0, tiles_part, square_rows, 0)
    turned = sqacc_v[...].T
    sq_v[mx] = total_of([turned[i * 8:(i + 1) * 8] for i in range(LANES // 8)])

    pl.semaphore_wait(barrier, nx + ny + nj - 3)
    sq_copies = []
    for d in range(1, nx):
        copy = pltpu.make_async_remote_copy(
            src_ref=sq_v.at[mx], dst_ref=sq_v.at[mx], send_sem=sq_send.at[d], recv_sem=sq_recv.at[mx],
            device_id={"ch": lax.rem(mx + d, nx)}, device_id_type=MESH)
        copy.start()
        sq_copies.append(copy)

    for copy in staged[:6]:
        copy.wait()
    step8 = lax.broadcasted_iota(jnp.int32, (8, LANES), 0).astype(F32)

    def rows_of(tile):
        return [jnp.broadcast_to(tile[m:m + 1, :], (8, LANES)) for m in range(modes)]

    def filter_block(b, carry):
        lanes = pl.ds(pl.multiple_of(b * LANES, LANES), LANES)
        rate = rate_v[:, lanes]
        weight = res_v[:, lanes] * jnp.sqrt(one_minus_exp_neg(2.0 * rate))
        jump = rows_of(jnp.exp(-8.0 * rate))
        terms = []
        for m in range(modes):
            power = jnp.exp(-rate[m:m + 1, :] * step8)
            pow_v[b * modes + m] = power
            terms.append(power * weight[m:m + 1, :])
        for t in range(tokens // 16):
            first = total_of(terms)
            terms = [a * c for a, c in zip(terms, jump)]
            second = total_of(terms)
            if t < tokens // 16 - 1:
                terms = [a * c for a, c in zip(terms, jump)]
            both = jnp.concatenate([first, second], axis=0)
            high = both.astype(BF16)
            taps_v[t * 16:(t + 1) * 16, lanes] = high
            taps_v[tokens + t * 16:tokens + (t + 1) * 16, lanes] = (both - high.astype(F32)).astype(BF16)
        return carry

    lax.fori_loop(0, blocks, filter_block, 0)

    for d in range(1, nx):
        src = lax.rem(mx + d, nx)
        pltpu.make_async_remote_copy(
            src_ref=sq_v.at[src], dst_ref=sq_v.at[src], send_sem=sq_send.at[d], recv_sem=sq_recv.at[src],
            device_id={"ch": src}, device_id_type=MESH).wait_recv()
    squares = jnp.sum(total_of([sq_v[i] for i in range(nx)]), axis=0, keepdims=True)
    scale = lax.rsqrt(squares / (nx * chans) + EPS)
    scol_v[...] = jnp.broadcast_to(scale, (tokens, LANES)).T

    def state_copy(b):
        return pltpu.make_async_remote_copy(
            src_ref=st_out.at[b], dst_ref=st_in.at[mj], send_sem=st_send.at[b], recv_sem=st_recv.at[mj],
            device_id=group_peer(b), device_id_type=MESH)

    def state_block(i, carry):
        b = lax.rem(mj + spread(i), nj)
        lanes = pl.ds(pl.multiple_of(b * LANES, LANES), LANES)
        rate = rate_v[:, lanes]
        jump = rows_of(jnp.exp(-8.0 * rate))
        gain = gain_v[pl.ds(b, 1), :]
        sums = [None] * modes
        for t in range(tokens // 16):
            value = x_v[t * 16:(t + 1) * 16, lanes].astype(F32) * scol_v[t * 16:(t + 1) * 16, :] * gain
            value = value.astype(BF16)
            xn_v[t * 16:(t + 1) * 16, lanes] = value
            value = value.astype(F32)
            for part in (value[:8], value[8:]):
                sums = [part if s is None else s * c + part for s, c in zip(sums, jump)]
        for m in range(modes):
            left = jnp.exp(-rate[m:m + 1, :] * (7.0 - step8))
            srow_v[m:m + 1, :] = jnp.sum(sums[m] * left, axis=0, keepdims=True)
        st_out[b] = srow_v[...].astype(st_out.dtype)

        @pl.when(i < nj - 1)
        def _():
            state_copy(b).start()

        return carry

    lax.fori_loop(0, nj, state_block, 0)
    st_in[mj] = st_out[mj]

    def local_conv(c, carry):
        lanes = pl.ds(pl.multiple_of(c * width, width), width)
        xn = xn_v[:, lanes]
        high = taps_v[:tokens, lanes]
        low = taps_v[tokens:, lanes]
        spec = jnp.dot(fwd_v[...], jnp.concatenate([xn, xn], axis=0), preferred_element_type=F32)
        filt = jnp.dot(fwd_v[...], jnp.concatenate([high, high], axis=0), preferred_element_type=F32)
        filt = filt + jnp.dot(fwd_v[:, :tokens], low, preferred_element_type=F32)
        xr, xi = spec[:tokens], spec[tokens:]
        fr, fi = filt[:tokens], filt[tokens:]
        prod = jnp.concatenate([xr * fr - xi * fi, xr * fi + xi * fr], axis=0)
        phigh = prod.astype(BF16)
        plow = (prod - phigh.astype(F32)).astype(BF16)
        conv = jnp.dot(inv_v[...], jnp.concatenate([phigh, phigh], axis=0), preferred_element_type=F32)
        conv = conv + jnp.dot(inv_v[:, :2 * tokens], plow, preferred_element_type=F32)
        per = width // LANES
        skip = jnp.concatenate([skip_v[pl.ds(c * per + n, 1), :] for n in range(per)], axis=1)
        conv_v[:, lanes] = conv + skip * xn.astype(F32)
        return carry

    chunks = chans // width
    cut1, cut2 = chunks // 2, (3 * chunks) // 4
    lax.fori_loop(0, cut1, local_conv, 0)

    own = pl.ds(pl.multiple_of(mj * LANES, LANES), LANES)
    rate = rate_v[:, own]
    decay = jnp.exp(-float(tokens) * rate)

    def scan_group(k, state):
        @pl.when(k != mj)
        def _():
            pltpu.make_async_remote_copy(
                src_ref=st_out.at[k], dst_ref=st_in.at[k], send_sem=st_send.at[k], recv_sem=st_recv.at[k],
                device_id=group_peer(k), device_id_type=MESH).wait_recv()

        pre_v[k] = state
        return state * decay + st_in[k].astype(F32)

    tot_v[my] = lax.fori_loop(0, nj, scan_group, jnp.zeros((modes, LANES), F32))

    tot_copies = []
    for d in range(1, ny):
        copy = pltpu.make_async_remote_copy(
            src_ref=tot_v.at[my], dst_ref=tot_v.at[my], send_sem=tot_send.at[d], recv_sem=tot_recv.at[my],
            device_id={"seq": lax.rem(seq + d * nj, ny * nj)}, device_id_type=MESH)
        copy.start()
        tot_copies.append(copy)

    lax.fori_loop(cut1, cut2, local_conv, 0)

    for d in range(1, ny):
        src = lax.rem(my + d, ny)
        pltpu.make_async_remote_copy(
            src_ref=tot_v.at[src], dst_ref=tot_v.at[src], send_sem=tot_send.at[d], recv_sem=tot_recv.at[src],
            device_id={"seq": src * nj + mj}, device_id_type=MESH).wait_recv()
    before = jnp.zeros((modes, LANES), F32)
    for k in range(ny):
        steps = jnp.maximum(my - 1 - k, 0) * (nj * tokens)
        live = (k < my).astype(F32)
        before = before + live * jnp.exp(-rate * steps.astype(F32)) * tot_v[k]
    scaled = res_v[:, own] * jnp.sqrt(one_minus_exp_neg(2.0 * rate)) * jnp.exp(-rate)

    def carry_copy(k):
        return pltpu.make_async_remote_copy(
            src_ref=ca_out.at[k], dst_ref=ca_in.at[mj], send_sem=ca_send.at[k], recv_sem=ca_recv.at[mj],
            device_id=group_peer(k), device_id_type=MESH)

    def send_carry(i, carry):
        k = lax.rem(mj + spread(i), nj)
        past = pre_v[k] + jnp.exp(-rate * (k * tokens).astype(F32)) * before
        ca_out[k] = (scaled * past).astype(ca_out.dtype)

        @pl.when(i < nj - 1)
        def _():
            carry_copy(k).start()

        return carry

    lax.fori_loop(0, nj, send_carry, 0)
    ca_in[mj] = ca_out[mj]

    lax.fori_loop(cut2, chunks, local_conv, 0)
    staged[6].wait()

    def finish_block(i, carry):
        b = lax.rem(mj + 2 * nj - spread(nj - 1 - i), nj)

        @pl.when(b != mj)
        def _():
            pltpu.make_async_remote_copy(
                src_ref=ca_out.at[b], dst_ref=ca_in.at[b], send_sem=ca_send.at[b], recv_sem=ca_recv.at[b],
                device_id=group_peer(b), device_id_type=MESH).wait_recv()

        lanes = pl.ds(pl.multiple_of(b * LANES, LANES), LANES)
        jump = rows_of(jnp.exp(-8.0 * rate_v[:, lanes]))
        weight = ca_in[b].astype(F32)
        terms = [pow_v[b * modes + m] * weight[m:m + 1, :] for m in range(modes)]
        for t in range(tokens // 16):
            first = total_of(terms)
            terms = [a * c for a, c in zip(terms, jump)]
            second = total_of(terms)
            if t < tokens // 16 - 1:
                terms = [a * c for a, c in zip(terms, jump)]
            both = jnp.concatenate([first, second], axis=0) + conv_v[t * 16:(t + 1) * 16, lanes]
            gate = gate_v[t * 16:(t + 1) * 16, lanes].astype(F32)
            out_ref[t * 16:(t + 1) * 16, lanes] = (both * gate).astype(BF16)
        return carry

    lax.fori_loop(0, blocks, finish_block, 0)

    for copy in sq_copies + tot_copies:
        copy.wait_send()

    def drain(k, carry):
        @pl.when(k != mj)
        def _():
            state_copy(k).wait_send()
            carry_copy(k).wait_send()

        return carry

    lax.fori_loop(0, nj, drain, 0)


def shards(nx, nseq, stream, norm_gain, gate_act, decay_rate, residue, skip_gain):
    tokens, chans = stream.shape
    modes = decay_rate.shape[1]
    blocks = chans // LANES
    nj = blocks
    ny = nseq // nj
    width = 256
    fwd, inv = half_tables(tokens)
    any_spec = pl.BlockSpec(memory_space=pl.ANY)
    vmem = pltpu.VMEM
    dma = pltpu.SemaphoreType.DMA
    return pl.pallas_call(
        functools.partial(kernel, nx, ny, nj, modes, width),
        out_shape=jax.ShapeDtypeStruct((tokens, chans), BF16),
        in_specs=[any_spec] * 8,
        out_specs=pl.BlockSpec(memory_space=pltpu.VMEM),
        scratch_shapes=[
            vmem((tokens, chans), BF16),
            vmem((tokens, chans), BF16),
            vmem((modes, chans), F32),
            vmem((modes, chans), F32),
            vmem((blocks, LANES), F32),
            vmem((blocks, LANES), F32),
            vmem(fwd.shape, BF16),
            vmem(inv.shape, BF16),
            vmem((tokens, LANES), F32),
            vmem((nx, 8, LANES), F32),
            vmem((tokens, LANES), F32),
            vmem((blocks * modes, 8, LANES), F32),
            vmem((2 * tokens, chans), BF16),
            vmem((tokens, chans), BF16),
            vmem((tokens, chans), F32),
            vmem((modes, LANES), F32),
            vmem((nj, modes, LANES), WIRE),
            vmem((nj, modes, LANES), WIRE),
            vmem((ny, modes, LANES), F32),
            vmem((nj, modes, LANES), F32),
            vmem((nj, modes, LANES), WIRE),
            vmem((nj, modes, LANES), WIRE),
            dma((7,)),
            dma((4,)),
            dma((nx,)),
            dma((nx,)),
            dma((nj,)),
            dma((nj,)),
            dma((ny,)),
            dma((ny,)),
            dma((nj,)),
            dma((nj,)),
        ],
        compiler_params=pltpu.CompilerParams(
            collective_id=0, has_side_effects=True, vmem_limit_bytes=32 * 1024 * 1024
        ),
    )(
        stream,
        decay_rate.T,
        residue.T,
        norm_gain.reshape(blocks, LANES),
        skip_gain.reshape(blocks, LANES),
        gate_act,
        jnp.asarray(fwd),
        jnp.asarray(inv),
    )


def solution(mesh):
    in_specs = (P("seq", "ch"), P("ch"), P("seq", "ch"), P("ch", None), P("ch", None), P("ch"))
    body = functools.partial(shards, mesh.shape["ch"], mesh.shape["seq"])
    return jax.shard_map(body, mesh=mesh, in_specs=in_specs, out_specs=P("seq", "ch"), check_vma=False)
```

```python
import functools
import math

import jax
import jax.numpy as jnp
import numpy as np
from jax import lax
from jax.experimental import pallas as pl
from jax.experimental.pallas import tpu as pltpu
from jax.sharding import PartitionSpec as P

MESH = pl.DeviceIdType.MESH
EPS = 1e-06
LANES = 128
WIRE = jnp.bfloat16
F32 = jnp.float32
BF16 = jnp.bfloat16


def half_tables(length):
    k = np.arange(length)[:, None] + 0.5
    t = np.arange(length)[None, :]
    angle = np.pi * k * t / length
    forward = np.concatenate([np.cos(angle), -np.sin(angle)], axis=0)
    inverse = np.concatenate([np.cos(angle.T), -np.sin(angle.T)], axis=1) / length

    def split(table):
        high = table.astype(BF16)
        low = (table - high.astype(np.float64)).astype(BF16)
        return np.concatenate([high, low], axis=1)

    return split(forward), split(inverse)


def one_minus_exp_neg(z):
    series = jnp.ones_like(z)
    for n in range(10, 1, -1):
        series = 1.0 - z * series * (1.0 / n)
    return jnp.where(z < 0.5, z * series, 1.0 - jnp.exp(-z))


def total_of(items):
    items = list(items)
    while len(items) > 1:
        items = [a + b for a, b in zip(items[::2], items[1::2])] + ([items[-1]] if len(items) % 2 else [])
    return items[0]


def kernel(nx, ny, nj, modes, width,
           x_hbm, rate_hbm, res_hbm, gain_hbm, skip_hbm, gate_hbm, fwd_hbm, inv_hbm, out_ref,
           x_v, gate_v, rate_v, res_v, gain_v, skip_v, fwd_v, inv_v,
           sqacc_v, sq_v, scol_v, pow_v, taps_v, xn_v, conv_v, srow_v,
           st_out, st_in, tot_v, pre_v, ca_out, ca_in,
           in_sem, x_sem, sq_send, sq_recv, st_send, st_recv, tot_send, tot_recv, ca_send, ca_recv):
    tokens, chans = x_v.shape
    blocks = chans // LANES
    mx = lax.axis_index("ch")
    seq = lax.axis_index("seq")
    my = seq // nj
    mj = lax.rem(seq, nj)

    def group_peer(k):
        return {"seq": my * nj + k}

    def spread(i):
        half = nj // 2
        return half + jnp.where(lax.rem(i, 2) == 1, (i + 1) // 2, -(i // 2))

    barrier = pltpu.get_barrier_semaphore()
    for d in range(1, nx):
        pl.semaphore_signal(barrier, inc=1, device_id={"ch": lax.rem(mx + d, nx)}, device_id_type=MESH)
    for d in range(1, ny):
        pl.semaphore_signal(barrier, inc=1, device_id={"seq": lax.rem(seq + d * nj, ny * nj)}, device_id_type=MESH)
    for d in range(1, nj):
        pl.semaphore_signal(barrier, inc=1, device_id=group_peer(lax.rem(mj + d, nj)), device_id_type=MESH)

    parts = x_sem.shape[0]
    rows_part = tokens // parts
    for p in range(parts):
        rows = pl.ds(p * rows_part, rows_part)
        pltpu.make_async_copy(x_hbm.at[rows], x_v.at[rows], x_sem.at[p]).start()
    staged = [(rate_hbm, rate_v), (res_hbm, res_v), (gain_hbm, gain_v), (skip_hbm, skip_v),
              (fwd_hbm, fwd_v), (inv_hbm, inv_v), (gate_hbm, gate_v)]
    staged = [pltpu.make_async_copy(a, b, in_sem.at[n]) for n, (a, b) in enumerate(staged)]
    for copy in staged:
        copy.start()

    tiles_part = rows_part // 16
    for p in range(parts):
        rows = pl.ds(p * rows_part, rows_part)
        pltpu.make_async_copy(x_hbm.at[rows], x_v.at[rows], x_sem.at[p]).wait()

        def square_rows(i, carry):
            part = pl.ds(pl.multiple_of(p * rows_part + i * 16, 16), 16)
            pieces = []
            for b in range(blocks):
                v = x_v[part, b * LANES:(b + 1) * LANES].astype(F32)
                pieces.append(v * v)
            sqacc_v[part, :] = total_of(pieces)
            return carry

        lax.fori_loop(0, tiles_part, square_rows, 0)
    turned = sqacc_v[...].T
    sq_v[mx] = total_of([turned[i * 8:(i + 1) * 8] for i in range(LANES // 8)])

    pl.semaphore_wait(barrier, nx + ny + nj - 3)
    sq_copies = []
    for d in range(1, nx):
        copy = pltpu.make_async_remote_copy(
            src_ref=sq_v.at[mx], dst_ref=sq_v.at[mx], send_sem=sq_send.at[d], recv_sem=sq_recv.at[mx],
            device_id={"ch": lax.rem(mx + d, nx)}, device_id_type=MESH)
        copy.start()
        sq_copies.append(copy)

    for copy in staged[:6]:
        copy.wait()
    step8 = lax.broadcasted_iota(jnp.int32, (8, LANES), 0).astype(F32)

    def rows_of(tile):
        return [jnp.broadcast_to(tile[m:m + 1, :], (8, LANES)) for m in range(modes)]

    def filter_block(b, carry):
        lanes = pl.ds(pl.multiple_of(b * LANES, LANES), LANES)
        rate = rate_v[:, lanes]
        weight = res_v[:, lanes] * jnp.sqrt(one_minus_exp_neg(2.0 * rate))
        jump = rows_of(jnp.exp(-8.0 * rate))
        terms = []
        for m in range(modes):
            power = jnp.exp(-rate[m:m + 1, :] * step8)
            pow_v[b * modes + m] = power
            terms.append(power * weight[m:m + 1, :])
        for t in range(tokens // 16):
            first = total_of(terms)
            terms = [a * c for a, c in zip(terms, jump)]
            second = total_of(terms)
            if t < tokens // 16 - 1:
                terms = [a * c for a, c in zip(terms, jump)]
            both = jnp.concatenate([first, second], axis=0)
            high = both.astype(BF16)
            taps_v[t * 16:(t + 1) * 16, lanes] = high
            taps_v[tokens + t * 16:tokens + (t + 1) * 16, lanes] = (both - high.astype(F32)).astype(BF16)
        return carry

    lax.fori_loop(0, blocks, filter_block, 0)

    for d in range(1, nx):
        src = lax.rem(mx + d, nx)
        pltpu.make_async_remote_copy(
            src_ref=sq_v.at[src], dst_ref=sq_v.at[src], send_sem=sq_send.at[d], recv_sem=sq_recv.at[src],
            device_id={"ch": src}, device_id_type=MESH).wait_recv()
    squares = jnp.sum(total_of([sq_v[i] for i in range(nx)]), axis=0, keepdims=True)
    scale = lax.rsqrt(squares / (nx * chans) + EPS)
    scol_v[...] = jnp.broadcast_to(scale, (tokens, LANES)).T

    def state_copy(b):
        return pltpu.make_async_remote_copy(
            src_ref=st_out.at[b], dst_ref=st_in.at[mj], send_sem=st_send.at[b], recv_sem=st_recv.at[mj],
            device_id=group_peer(b), device_id_type=MESH)

    def state_block(i, carry):
        b = lax.rem(mj + spread(i), nj)
        lanes = pl.ds(pl.multiple_of(b * LANES, LANES), LANES)
        rate = rate_v[:, lanes]
        jump = rows_of(jnp.exp(-8.0 * rate))
        gain = gain_v[pl.ds(b, 1), :]
        sums = [None] * modes
        for t in range(tokens // 16):
            value = x_v[t * 16:(t + 1) * 16, lanes].astype(F32) * scol_v[t * 16:(t + 1) * 16, :] * gain
            value = value.astype(BF16)
            xn_v[t * 16:(t + 1) * 16, lanes] = value
            value = value.astype(F32)
            for part in (value[:8], value[8:]):
                sums = [part if s is None else s * c + part for s, c in zip(sums, jump)]
        for m in range(modes):
            left = jnp.exp(-rate[m:m + 1, :] * (7.0 - step8))
            srow_v[m:m + 1, :] = jnp.sum(sums[m] * left, axis=0, keepdims=True)
        st_out[b] = srow_v[...].astype(st_out.dtype)

        @pl.when(i < nj - 1)
        def _():
            state_copy(b).start()

        return carry

    lax.fori_loop(0, nj, state_block, 0)
    st_in[mj] = st_out[mj]

    def local_conv(c, carry):
        lanes = pl.ds(pl.multiple_of(c * width, width), width)
        xn = xn_v[:, lanes]
        high = taps_v[:tokens, lanes]
        low = taps_v[tokens:, lanes]
        spec = jnp.dot(fwd_v[...], jnp.concatenate([xn, xn], axis=0), preferred_element_type=F32)
        filt = jnp.dot(fwd_v[...], jnp.concatenate([high, high], axis=0), preferred_element_type=F32)
        filt = filt + jnp.dot(fwd_v[:, :tokens], low, preferred_element_type=F32)
        xr, xi = spec[:tokens], spec[tokens:]
        fr, fi = filt[:tokens], filt[tokens:]
        prod = jnp.concatenate([xr * fr - xi * fi, xr * fi + xi * fr], axis=0)
        phigh = prod.astype(BF16)
        plow = (prod - phigh.astype(F32)).astype(BF16)
        conv = jnp.dot(inv_v[...], jnp.concatenate([phigh, phigh], axis=0), preferred_element_type=F32)
        conv = conv + jnp.dot(inv_v[:, :2 * tokens], plow, preferred_element_type=F32)
        per = width // LANES
        skip = jnp.concatenate([skip_v[pl.ds(c * per + n, 1), :] for n in range(per)], axis=1)
        conv_v[:, lanes] = conv + skip * xn.astype(F32)
        return carry

    chunks = chans // width
    cut1, cut2 = chunks // 2, (3 * chunks) // 4
    lax.fori_loop(0, cut1, local_conv, 0)

    own = pl.ds(pl.multiple_of(mj * LANES, LANES), LANES)
    rate = rate_v[:, own]
    decay = jnp.exp(-float(tokens) * rate)

    def scan_group(k, state):
        @pl.when(k != mj)
        def _():
            pltpu.make_async_remote_copy(
                src_ref=st_out.at[k], dst_ref=st_in.at[k], send_sem=st_send.at[k], recv_sem=st_recv.at[k],
                device_id=group_peer(k), device_id_type=MESH).wait_recv()

        pre_v[k] = state
        return state * decay + st_in[k].astype(F32)

    tot_v[my] = lax.fori_loop(0, nj, scan_group, jnp.zeros((modes, LANES), F32))

    tot_copies = []
    for d in range(1, ny):
        copy = pltpu.make_async_remote_copy(
            src_ref=tot_v.at[my], dst_ref=tot_v.at[my], send_sem=tot_send.at[d], recv_sem=tot_recv.at[my],
            device_id={"seq": lax.rem(seq + d * nj, ny * nj)}, device_id_type=MESH)
        copy.start()
        tot_copies.append(copy)

    lax.fori_loop(cut1, cut2, local_conv, 0)

    for d in range(1, ny):
        src = lax.rem(my + d, ny)
        pltpu.make_async_remote_copy(
            src_ref=tot_v.at[src], dst_ref=tot_v.at[src], send_sem=tot_send.at[d], recv_sem=tot_recv.at[src],
            device_id={"seq": src * nj + mj}, device_id_type=MESH).wait_recv()
    before = jnp.zeros((modes, LANES), F32)
    for k in range(ny):
        steps = jnp.maximum(my - 1 - k, 0) * (nj * tokens)
        live = (k < my).astype(F32)
        before = before + live * jnp.exp(-rate * steps.astype(F32)) * tot_v[k]
    scaled = res_v[:, own] * jnp.sqrt(one_minus_exp_neg(2.0 * rate)) * jnp.exp(-rate)

    def carry_copy(k):
        return pltpu.make_async_remote_copy(
            src_ref=ca_out.at[k], dst_ref=ca_in.at[mj], send_sem=ca_send.at[k], recv_sem=ca_recv.at[mj],
            device_id=group_peer(k), device_id_type=MESH)

    def send_carry(i, carry):
        k = lax.rem(mj + spread(i), nj)
        past = pre_v[k] + jnp.exp(-rate * (k * tokens).astype(F32)) * before
        ca_out[k] = (scaled * past).astype(ca_out.dtype)

        @pl.when(i < nj - 1)
        def _():
            carry_copy(k).start()

        return carry

    lax.fori_loop(0, nj, send_carry, 0)
    ca_in[mj] = ca_out[mj]

    lax.fori_loop(cut2, chunks, local_conv, 0)
    staged[6].wait()

    def finish_block(i, carry):
        b = lax.rem(mj + 2 * nj - spread(nj - 1 - i), nj)

        @pl.when(b != mj)
        def _():
            pltpu.make_async_remote_copy(
                src_ref=ca_out.at[b], dst_ref=ca_in.at[b], send_sem=ca_send.at[b], recv_sem=ca_recv.at[b],
                device_id=group_peer(b), device_id_type=MESH).wait_recv()

        lanes = pl.ds(pl.multiple_of(b * LANES, LANES), LANES)
        jump = rows_of(jnp.exp(-8.0 * rate_v[:, lanes]))
        weight = ca_in[b].astype(F32)
        terms = [pow_v[b * modes + m] * weight[m:m + 1, :] for m in range(modes)]
        for t in range(tokens // 16):
            first = total_of(terms)
            terms = [a * c for a, c in zip(terms, jump)]
            second = total_of(terms)
            if t < tokens // 16 - 1:
                terms = [a * c for a, c in zip(terms, jump)]
            both = jnp.concatenate([first, second], axis=0) + conv_v[t * 16:(t + 1) * 16, lanes]
            gate = gate_v[t * 16:(t + 1) * 16, lanes].astype(F32)
            out_ref[t * 16:(t + 1) * 16, lanes] = (both * gate).astype(BF16)
        return carry

    lax.fori_loop(0, blocks, finish_block, 0)

    for copy in sq_copies + tot_copies:
        copy.wait_send()

    def drain(k, carry):
        @pl.when(k != mj)
        def _():
            state_copy(k).wait_send()
            carry_copy(k).wait_send()

        return carry

    lax.fori_loop(0, nj, drain, 0)


def shards(nx, nseq, stream, norm_gain, gate_act, decay_rate, residue, skip_gain):
    tokens, chans = stream.shape
    modes = decay_rate.shape[1]
    blocks = chans // LANES
    nj = blocks
    ny = nseq // nj
    width = 256
    fwd, inv = half_tables(tokens)
    any_spec = pl.BlockSpec(memory_space=pl.ANY)
    vmem = pltpu.VMEM
    dma = pltpu.SemaphoreType.DMA
    return pl.pallas_call(
        functools.partial(kernel, nx, ny, nj, modes, width),
        out_shape=jax.ShapeDtypeStruct((tokens, chans), BF16),
        in_specs=[any_spec] * 8,
        out_specs=pl.BlockSpec(memory_space=pltpu.VMEM),
        scratch_shapes=[
            vmem((tokens, chans), BF16),
            vmem((tokens, chans), BF16),
            vmem((modes, chans), F32),
            vmem((modes, chans), F32),
            vmem((blocks, LANES), F32),
            vmem((blocks, LANES), F32),
            vmem(fwd.shape, BF16),
            vmem(inv.shape, BF16),
            vmem((tokens, LANES), F32),
            vmem((nx, 8, LANES), F32),
            vmem((tokens, LANES), F32),
            vmem((blocks * modes, 8, LANES), F32),
            vmem((2 * tokens, chans), BF16),
            vmem((tokens, chans), BF16),
            vmem((tokens, chans), F32),
            vmem((modes, LANES), F32),
            vmem((nj, modes, LANES), WIRE),
            vmem((nj, modes, LANES), WIRE),
            vmem((ny, modes, LANES), F32),
            vmem((nj, modes, LANES), F32),
            vmem((nj, modes, LANES), WIRE),
            vmem((nj, modes, LANES), WIRE),
            dma((7,)),
            dma((4,)),
            dma((nx,)),
            dma((nx,)),
            dma((nj,)),
            dma((nj,)),
            dma((ny,)),
            dma((ny,)),
            dma((nj,)),
            dma((nj,)),
        ],
        compiler_params=pltpu.CompilerParams(
            collective_id=0, has_side_effects=True, vmem_limit_bytes=40 * 1024 * 1024
        ),
    )(*[pltpu.with_memory_space_constraint(v, pltpu.HBM) for v in (
        stream,
        decay_rate.T,
        residue.T,
        norm_gain.reshape(blocks, LANES),
        skip_gain.reshape(blocks, LANES),
        gate_act,
        jnp.asarray(fwd),
        jnp.asarray(inv),
    )])


def solution(mesh):
    in_specs = (P("seq", "ch"), P("ch"), P("seq", "ch"), P("ch", None), P("ch", None), P("ch"))
    body = functools.partial(shards, mesh.shape["ch"], mesh.shape["seq"])
    return jax.shard_map(body, mesh=mesh, in_specs=in_specs, out_specs=P("seq", "ch"), check_vma=False)
```

```python
import functools
import math

import jax
import jax.numpy as jnp
import numpy as np
from jax import lax
from jax.experimental import pallas as pl
from jax.experimental.pallas import tpu as pltpu
from jax.sharding import PartitionSpec as P

MESH = pl.DeviceIdType.MESH
EPS = 1e-06
LANES = 128
WIRE = jnp.bfloat16
CHIPS_Y = 4
F32 = jnp.float32
BF16 = jnp.bfloat16


def half_tables(length):
    k = np.arange(length)[:, None] + 0.5
    t = np.arange(length)[None, :]
    angle = np.pi * k * t / length
    forward = np.concatenate([np.cos(angle), -np.sin(angle)], axis=0)
    inverse = np.concatenate([np.cos(angle.T), -np.sin(angle.T)], axis=1) / length

    def split(table):
        high = table.astype(BF16)
        low = (table - high.astype(np.float64)).astype(BF16)
        return np.concatenate([high, low], axis=1)

    return split(forward), split(inverse)


def one_minus_exp_neg(z):
    series = jnp.ones_like(z)
    for n in range(10, 1, -1):
        series = 1.0 - z * series * (1.0 / n)
    return jnp.where(z < 0.5, z * series, 1.0 - jnp.exp(-z))


def total_of(items):
    items = list(items)
    while len(items) > 1:
        items = [a + b for a, b in zip(items[::2], items[1::2])] + ([items[-1]] if len(items) % 2 else [])
    return items[0]


def kernel(nx, ny, nz, modes, width,
           x_hbm, rate_hbm, res_hbm, gain_hbm, skip_hbm, gate_hbm, fwd_hbm, inv_hbm, out_ref,
           x_v, gate_v, rate_v, res_v, gain_v, skip_v, fwd_v, inv_v,
           sqacc_v, sq_v, scol_v, pow_v, taps_v, xn_v, conv_v, srow_v, wa_v,
           pair_out, pair_in, st_out, st_in, ca_out, ca_in,
           in_sem, x_sem, sq_send, sq_recv, pair_send, pair_recv, st_send, st_recv, ca_send, ca_recv):
    tokens, chans = x_v.shape
    blocks = chans // LANES
    nchips = ny * nz
    half = modes // 2
    mx = lax.axis_index("ch")
    seq = lax.axis_index("seq")
    chip = seq // 2
    core = lax.rem(seq, 2)
    my = chip // nz
    mp = lax.rem(chip, nz) // 2

    def chip_peer(q):
        return {"seq": q * 2 + core}

    partner = {"seq": chip * 2 + 1 - core}

    def spread(n, i):
        return n // 2 + jnp.where(lax.rem(i, 2) == 1, (i + 1) // 2, -(i // 2))

    def block_of(i):
        py = lax.rem(my + spread(ny, lax.rem(i, ny)), ny)
        pz = lax.rem(mp + spread(nz // 2, i // ny), nz // 2)
        return py * (nz // 2) + pz

    barrier = pltpu.get_barrier_semaphore()
    for d in range(1, nx):
        pl.semaphore_signal(barrier, inc=1, device_id={"ch": lax.rem(mx + d, nx)}, device_id_type=MESH)
    pl.semaphore_signal(barrier, inc=1, device_id=partner, device_id_type=MESH)

    def greet(d, carry):
        pl.semaphore_signal(barrier, inc=1, device_id=chip_peer(lax.rem(chip + d, nchips)), device_id_type=MESH)
        return carry

    lax.fori_loop(1, nchips, greet, 0)

    parts = x_sem.shape[0]
    rows_part = tokens // parts
    for p in range(parts):
        rows = pl.ds(p * rows_part, rows_part)
        pltpu.make_async_copy(x_hbm.at[rows], x_v.at[rows], x_sem.at[p]).start()
    staged = [(rate_hbm, rate_v), (res_hbm, res_v), (gain_hbm, gain_v), (skip_hbm, skip_v),
              (fwd_hbm, fwd_v), (inv_hbm, inv_v), (gate_hbm, gate_v)]
    staged = [pltpu.make_async_copy(a, b, in_sem.at[n]) for n, (a, b) in enumerate(staged)]
    for copy in staged:
        copy.start()

    tiles_part = rows_part // 16
    for p in range(parts):
        rows = pl.ds(p * rows_part, rows_part)
        pltpu.make_async_copy(x_hbm.at[rows], x_v.at[rows], x_sem.at[p]).wait()

        def square_rows(i, carry):
            part = pl.ds(pl.multiple_of(p * rows_part + i * 16, 16), 16)
            pieces = []
            for b in range(blocks):
                v = x_v[part, b * LANES:(b + 1) * LANES].astype(F32)
                pieces.append(v * v)
            sqacc_v[part, :] = total_of(pieces)
            return carry

        lax.fori_loop(0, tiles_part, square_rows, 0)
    turned = sqacc_v[...].T
    sq_v[mx] = total_of([turned[i * 8:(i + 1) * 8] for i in range(LANES // 8)])

    pl.semaphore_wait(barrier, nx + nchips - 1)
    sq_copies = []
    for d in range(1, nx):
        copy = pltpu.make_async_remote_copy(
            src_ref=sq_v.at[mx], dst_ref=sq_v.at[mx], send_sem=sq_send.at[d], recv_sem=sq_recv.at[mx],
            device_id={"ch": lax.rem(mx + d, nx)}, device_id_type=MESH)
        copy.start()
        sq_copies.append(copy)

    for copy in staged[:6]:
        copy.wait()
    step8 = lax.broadcasted_iota(jnp.int32, (8, LANES), 0).astype(F32)

    def rows_of(tile):
        return [jnp.broadcast_to(tile[m:m + 1, :], (8, LANES)) for m in range(modes)]

    def filter_block(b, carry):
        lanes = pl.ds(pl.multiple_of(b * LANES, LANES), LANES)
        rate = rate_v[:, lanes]
        weight = res_v[:, lanes] * jnp.sqrt(one_minus_exp_neg(2.0 * rate))
        wa_v[:, lanes] = weight * jnp.exp(-rate)
        jump = rows_of(jnp.exp(-8.0 * rate))
        terms = []
        for m in range(modes):
            power = jnp.exp(-rate[m:m + 1, :] * step8)
            pow_v[b * modes + m] = power
            terms.append(power * weight[m:m + 1, :])
        for t in range(tokens // 16):
            first = total_of(terms)
            terms = [a * c for a, c in zip(terms, jump)]
            second = total_of(terms)
            if t < tokens // 16 - 1:
                terms = [a * c for a, c in zip(terms, jump)]
            both = jnp.concatenate([first, second], axis=0)
            high = both.astype(BF16)
            taps_v[t * 16:(t + 1) * 16, lanes] = high
            taps_v[tokens + t * 16:tokens + (t + 1) * 16, lanes] = (both - high.astype(F32)).astype(BF16)
        return carry

    lax.fori_loop(0, blocks, filter_block, 0)

    for d in range(1, nx):
        src = lax.rem(mx + d, nx)
        pltpu.make_async_remote_copy(
            src_ref=sq_v.at[src], dst_ref=sq_v.at[src], send_sem=sq_send.at[d], recv_sem=sq_recv.at[src],
            device_id={"ch": src}, device_id_type=MESH).wait_recv()
    squares = jnp.sum(total_of([sq_v[i] for i in range(nx)]), axis=0, keepdims=True)
    scale = lax.rsqrt(squares / (nx * chans) + EPS)
    scol_v[...] = jnp.broadcast_to(scale, (tokens, LANES)).T

    batch = blocks // pair_send.shape[0]

    def pair_copy(g):
        slots = pl.ds(g * batch, batch)
        return pltpu.make_async_remote_copy(
            src_ref=pair_out.at[slots], dst_ref=pair_in.at[slots], send_sem=pair_send.at[g], recv_sem=pair_recv.at[g],
            device_id=partner, device_id_type=MESH)

    def state_block(i, carry):
        b = block_of(i)
        lanes = pl.ds(pl.multiple_of(b * LANES, LANES), LANES)
        rate = rate_v[:, lanes]
        jump = rows_of(jnp.exp(-8.0 * rate))
        gain = gain_v[pl.ds(b, 1), :]
        sums = [None] * modes
        for t in range(tokens // 16):
            value = x_v[t * 16:(t + 1) * 16, lanes].astype(F32) * scol_v[t * 16:(t + 1) * 16, :] * gain
            value = value.astype(BF16)
            xn_v[t * 16:(t + 1) * 16, lanes] = value
            value = value.astype(F32)
            for part in (value[:8], value[8:]):
                sums = [part if s is None else s * c + part for s, c in zip(sums, jump)]
        for m in range(modes):
            left = jnp.exp(-rate[m:m + 1, :] * (7.0 - step8))
            srow_v[m:m + 1, :] = jnp.sum(sums[m] * left, axis=0, keepdims=True)
        pair_out[i] = srow_v[...]

        @pl.when(lax.rem(i, batch) == batch - 1)
        def _():
            pair_copy(i // batch).start()

        return carry

    lax.fori_loop(0, blocks, state_block, 0)

    def state_copy(q):
        return pltpu.make_async_remote_copy(
            src_ref=st_out.at[q], dst_ref=st_in.at[chip], send_sem=st_send.at[q], recv_sem=st_recv.at[chip],
            device_id=chip_peer(q), device_id_type=MESH)

    def join_block(i, carry):
        @pl.when(lax.rem(i, batch) == 0)
        def _():
            pair_copy(i // batch).wait_recv()

        b = block_of(i)
        decay = jnp.exp(-float(tokens) * rate_v[:, pl.ds(pl.multiple_of(b * LANES, LANES), LANES)])
        mine, other = pair_out[i], pair_in[i]
        joined = jnp.where(core == 0, mine * decay + other, other * decay + mine)
        st_out[2 * b] = joined[:half].astype(st_out.dtype)
        st_out[2 * b + 1] = joined[half:].astype(st_out.dtype)
        for n in range(2):
            @pl.when(2 * b + n != chip)
            def _():
                state_copy(2 * b + n).start()

        return carry

    lax.fori_loop(0, blocks, join_block, 0)
    st_in[chip] = st_out[chip]

    def local_conv(c, carry):
        lanes = pl.ds(pl.multiple_of(c * width, width), width)
        xn = xn_v[:, lanes]
        high = taps_v[:tokens, lanes]
        low = taps_v[tokens:, lanes]
        spec = jnp.dot(fwd_v[...], jnp.concatenate([xn, xn], axis=0), preferred_element_type=F32)
        filt = jnp.dot(fwd_v[...], jnp.concatenate([high, high], axis=0), preferred_element_type=F32)
        filt = filt + jnp.dot(fwd_v[:, :tokens], low, preferred_element_type=F32)
        xr, xi = spec[:tokens], spec[tokens:]
        fr, fi = filt[:tokens], filt[tokens:]
        prod = jnp.concatenate([xr * fr - xi * fi, xr * fi + xi * fr], axis=0)
        phigh = prod.astype(BF16)
        plow = (prod - phigh.astype(F32)).astype(BF16)
        conv = jnp.dot(inv_v[...], jnp.concatenate([phigh, phigh], axis=0), preferred_element_type=F32)
        conv = conv + jnp.dot(inv_v[:, :2 * tokens], plow, preferred_element_type=F32)
        per = width // LANES
        skip = jnp.concatenate([skip_v[pl.ds(c * per + n, 1), :] for n in range(per)], axis=1)
        conv_v[:, lanes] = conv + skip * xn.astype(F32)
        return carry

    chunks = chans // width
    cut1 = chunks // 2
    lax.fori_loop(0, cut1, local_conv, 0)

    own = pl.ds(pl.multiple_of((chip // 2) * LANES, LANES), LANES)
    rate = rate_v[pl.ds(pl.multiple_of(lax.rem(chip, 2) * half, half), half), own]
    decay = jnp.exp(-float(2 * tokens) * rate)

    def scan_chips(q, state):
        @pl.when(q != chip)
        def _():
            pltpu.make_async_remote_copy(
                src_ref=st_out.at[q], dst_ref=st_in.at[q], send_sem=st_send.at[q], recv_sem=st_recv.at[q],
                device_id=chip_peer(q), device_id_type=MESH).wait_recv()

        ca_out[q] = state.astype(ca_out.dtype)
        return state * decay + st_in[q].astype(F32)

    lax.fori_loop(0, nchips, scan_chips, jnp.zeros((half, LANES), F32))

    def carry_copy(q):
        return pltpu.make_async_remote_copy(
            src_ref=ca_out.at[q], dst_ref=ca_in.at[chip], send_sem=ca_send.at[q], recv_sem=ca_recv.at[chip],
            device_id=chip_peer(q), device_id_type=MESH)

    def send_carry(i, carry):
        q = lax.rem(i, ny) * nz + i // ny

        @pl.when(q != chip)
        def _():
            carry_copy(q).start()

        return carry

    lax.fori_loop(0, nchips, send_carry, 0)
    ca_in[chip] = ca_out[chip]

    lax.fori_loop(cut1, chunks, local_conv, 0)
    staged[6].wait()

    def finish_block(i, carry):
        slot = blocks - 1 - i
        b = block_of(slot)
        for n in range(2):
            q = 2 * b + n

            @pl.when(q != chip)
            def _():
                pltpu.make_async_remote_copy(
                    src_ref=ca_out.at[q], dst_ref=ca_in.at[q], send_sem=ca_send.at[q], recv_sem=ca_recv.at[q],
                    device_id=chip_peer(q), device_id_type=MESH).wait_recv()

        lanes = pl.ds(pl.multiple_of(b * LANES, LANES), LANES)
        rate = rate_v[:, lanes]
        jump = rows_of(jnp.exp(-8.0 * rate))
        past = jnp.concatenate([ca_in[2 * b].astype(F32), ca_in[2 * b + 1].astype(F32)], axis=0)
        past = jnp.where(core == 0, past, past * jnp.exp(-float(tokens) * rate) + pair_in[slot])
        weight = past * wa_v[:, lanes]
        terms = [pow_v[b * modes + m] * weight[m:m + 1, :] for m in range(modes)]
        for t in range(tokens // 16):
            first = total_of(terms)
            terms = [a * c for a, c in zip(terms, jump)]
            second = total_of(terms)
            if t < tokens // 16 - 1:
                terms = [a * c for a, c in zip(terms, jump)]
            both = jnp.concatenate([first, second], axis=0) + conv_v[t * 16:(t + 1) * 16, lanes]
            gate = gate_v[t * 16:(t + 1) * 16, lanes].astype(F32)
            out_ref[t * 16:(t + 1) * 16, lanes] = (both * gate).astype(BF16)
        return carry

    lax.fori_loop(0, blocks, finish_block, 0)

    for copy in sq_copies:
        copy.wait_send()
    for g in range(pair_send.shape[0]):
        pair_copy(g).wait_send()

    def drain(q, carry):
        @pl.when(q != chip)
        def _():
            state_copy(q).wait_send()
            carry_copy(q).wait_send()

        return carry

    lax.fori_loop(0, nchips, drain, 0)


def shards(nx, nseq, stream, norm_gain, gate_act, decay_rate, residue, skip_gain):
    tokens, chans = stream.shape
    modes = decay_rate.shape[1]
    blocks = chans // LANES
    nchips = nseq // 2
    ny = CHIPS_Y
    nz = nchips // ny
    width = 256
    pairs = min(4, blocks)
    fwd, inv = half_tables(tokens)
    any_spec = pl.BlockSpec(memory_space=pl.ANY)
    vmem = pltpu.VMEM
    dma = pltpu.SemaphoreType.DMA
    return pl.pallas_call(
        functools.partial(kernel, nx, ny, nz, modes, width),
        out_shape=jax.ShapeDtypeStruct((tokens, chans), BF16),
        in_specs=[any_spec] * 8,
        out_specs=pl.BlockSpec(memory_space=pltpu.VMEM),
        scratch_shapes=[
            vmem((tokens, chans), BF16),
            vmem((tokens, chans), BF16),
            vmem((modes, chans), F32),
            vmem((modes, chans), F32),
            vmem((blocks, LANES), F32),
            vmem((blocks, LANES), F32),
            vmem(fwd.shape, BF16),
            vmem(inv.shape, BF16),
            vmem((tokens, LANES), F32),
            vmem((nx, 8, LANES), F32),
            vmem((tokens, LANES), F32),
            vmem((blocks * modes, 8, LANES), F32),
            vmem((2 * tokens, chans), BF16),
            vmem((tokens, chans), BF16),
            vmem((tokens, chans), F32),
            vmem((modes, LANES), F32),
            vmem((modes, chans), F32),
            vmem((blocks, modes, LANES), F32),
            vmem((blocks, modes, LANES), F32),
            vmem((nchips, modes // 2, LANES), WIRE),
            vmem((nchips, modes // 2, LANES), WIRE),
            vmem((nchips, modes // 2, LANES), WIRE),
            vmem((nchips, modes // 2, LANES), WIRE),
            dma((7,)),
            dma((4,)),
            dma((nx,)),
            dma((nx,)),
            dma((pairs,)),
            dma((pairs,)),
            dma((nchips,)),
            dma((nchips,)),
            dma((nchips,)),
            dma((nchips,)),
        ],
        compiler_params=pltpu.CompilerParams(
            collective_id=0, has_side_effects=True, vmem_limit_bytes=40 * 1024 * 1024
        ),
    )(*[pltpu.with_memory_space_constraint(v, pltpu.HBM) for v in (
        stream,
        decay_rate.T,
        residue.T,
        norm_gain.reshape(blocks, LANES),
        skip_gain.reshape(blocks, LANES),
        gate_act,
        jnp.asarray(fwd),
        jnp.asarray(inv),
    )])


def solution(mesh):
    in_specs = (P("seq", "ch"), P("ch"), P("seq", "ch"), P("ch", None), P("ch", None), P("ch"))
    body = functools.partial(shards, mesh.shape["ch"], mesh.shape["seq"])
    return jax.shard_map(body, mesh=mesh, in_specs=in_specs, out_specs=P("seq", "ch"), check_vma=False)
```

```python
import functools
import math

import jax
import jax.numpy as jnp
import numpy as np
from jax import lax
from jax.experimental import pallas as pl
from jax.experimental.pallas import tpu as pltpu
from jax.sharding import PartitionSpec as P

MESH = pl.DeviceIdType.MESH
EPS = 1e-06
LANES = 128
WIRE = jnp.bfloat16
F32 = jnp.float32
BF16 = jnp.bfloat16


def half_tables(length):
    k = np.arange(length)[:, None] + 0.5
    t = np.arange(length)[None, :]
    angle = np.pi * k * t / length
    forward = np.concatenate([np.cos(angle), -np.sin(angle)], axis=0)
    inverse = np.concatenate([np.cos(angle.T), -np.sin(angle.T)], axis=1) / length

    def split(table):
        high = table.astype(BF16)
        low = (table - high.astype(np.float64)).astype(BF16)
        return np.concatenate([high, low], axis=1)

    return split(forward), split(inverse)


def one_minus_exp_neg(z):
    series = jnp.ones_like(z)
    for n in range(10, 1, -1):
        series = 1.0 - z * series * (1.0 / n)
    return jnp.where(z < 0.5, z * series, 1.0 - jnp.exp(-z))


def total_of(items):
    items = list(items)
    while len(items) > 1:
        items = [a + b for a, b in zip(items[::2], items[1::2])] + ([items[-1]] if len(items) % 2 else [])
    return items[0]


def rows_of(tile):
    return [jnp.broadcast_to(tile[m:m + 1, :], (8, LANES)) for m in range(tile.shape[0])]


def row_sums(tiles):
    row = lax.broadcasted_iota(jnp.int32, (8, LANES), 0)
    for bit in (4, 2, 1):
        clear = lax.rem(row // bit, 2) == 0
        count = len(tiles) // 2
        tiles = [jnp.where(clear, a + pltpu.roll(a, 8 - bit, 0), c + pltpu.roll(c, bit, 0))
                 for a, c in zip(tiles[:count], tiles[count:])]
    return tiles[0]


def kernel(nx, ny, nj, modes, width,
           x_hbm, rate_hbm, res_hbm, gain_hbm, skip_hbm, gate_hbm, fwd_hbm, inv_hbm, out_ref,
           x_v, gate_v, rate_v, res_v, gain_v, skip_v, fwd_v, inv_v,
           sqacc_v, sq_v, scol_v, pow_v, taps_v, xn_v, conv_v, left_v, jump_v,
           st_out, st_in, tot_v, pre_v, ca_out, ca_in,
           in_sem, x_sem, sq_send, sq_recv, st_send, st_recv, tot_send, tot_recv, ca_send, ca_recv):
    tokens, chans = x_v.shape
    blocks = chans // LANES
    mx = lax.axis_index("ch")
    seq = lax.axis_index("seq")
    my = seq // nj
    mj = lax.rem(seq, nj)

    def group_peer(k):
        return {"seq": my * nj + k}

    def spread(i):
        return nj // 2 + jnp.where(lax.rem(i, 2) == 1, (i + 1) // 2, -(i // 2))

    parts = x_sem.shape[0]
    rows_part = tokens // parts
    for p in range(parts):
        rows = pl.ds(p * rows_part, rows_part)
        pltpu.make_async_copy(x_hbm.at[rows], x_v.at[rows], x_sem.at[p]).start()
    staged = [(rate_hbm, rate_v), (res_hbm, res_v), (gain_hbm, gain_v), (skip_hbm, skip_v),
              (fwd_hbm, fwd_v), (inv_hbm, inv_v), (gate_hbm, gate_v)]
    staged = [pltpu.make_async_copy(a, b, in_sem.at[n]) for n, (a, b) in enumerate(staged)]
    for copy in staged:
        copy.start()

    half = nj // 2
    late = mj >= half
    barrier = pltpu.get_barrier_semaphore()
    for d in range(1, nx):
        pl.semaphore_signal(barrier, inc=1, device_id={"ch": lax.rem(mx + d, nx)}, device_id_type=MESH)
    for d in range(1, ny):
        pl.semaphore_signal(barrier, inc=1, device_id={"seq": lax.rem(seq + d * nj, ny * nj)}, device_id_type=MESH)

    def greet(first):
        for k in range(first, first + half):
            @pl.when(k != mj)
            def _():
                pl.semaphore_signal(barrier, inc=1, device_id=group_peer(k), device_id_type=MESH)

    @pl.when(late)
    def _():
        greet(half)

    tiles_part = rows_part // 16
    for p in range(parts):
        rows = pl.ds(p * rows_part, rows_part)
        pltpu.make_async_copy(x_hbm.at[rows], x_v.at[rows], x_sem.at[p]).wait()

        def square_rows(i, carry):
            part = pl.ds(pl.multiple_of(p * rows_part + i * 16, 16), 16)
            pieces = []
            for b in range(blocks):
                v = x_v[part, b * LANES:(b + 1) * LANES].astype(F32)
                pieces.append(v * v)
            sqacc_v[part, :] = total_of(pieces)
            return carry

        lax.fori_loop(0, tiles_part, square_rows, 0)
    turned = sqacc_v[...].T
    sq_v[mx] = total_of([turned[i * 8:(i + 1) * 8] for i in range(LANES // 8)])

    @pl.when(late)
    def _():
        pl.semaphore_wait(barrier, nx + ny + nj - 3)
        greet(0)

    @pl.when(jnp.logical_not(late))
    def _():
        pl.semaphore_wait(barrier, nx + ny - 2)
        greet(half)

    sq_copies = []
    for d in range(1, nx):
        copy = pltpu.make_async_remote_copy(
            src_ref=sq_v.at[mx], dst_ref=sq_v.at[mx], send_sem=sq_send.at[d], recv_sem=sq_recv.at[mx],
            device_id={"ch": lax.rem(mx + d, nx)}, device_id_type=MESH)
        copy.start()
        sq_copies.append(copy)

    for copy in staged[:6]:
        copy.wait()
    step8 = lax.broadcasted_iota(jnp.int32, (8, LANES), 0).astype(F32)

    def filter_block(b, carry):
        lanes = pl.ds(pl.multiple_of(b * LANES, LANES), LANES)
        rate = rate_v[:, lanes]
        weight = res_v[:, lanes] * jnp.sqrt(one_minus_exp_neg(2.0 * rate))
        jump = jnp.exp(-8.0 * rate)
        jump_v[:, lanes] = jump
        jump = rows_of(jump)
        terms = []
        for m in range(modes):
            power = jnp.exp(-rate[m:m + 1, :] * step8)
            pow_v[b * modes + m] = power
            left_v[b * modes + m] = jnp.exp(-rate[m:m + 1, :] * (7.0 - step8))
            terms.append(power * weight[m:m + 1, :])
        for t in range(tokens // 16):
            first = total_of(terms)
            terms = [a * c for a, c in zip(terms, jump)]
            second = total_of(terms)
            if t < tokens // 16 - 1:
                terms = [a * c for a, c in zip(terms, jump)]
            both = jnp.concatenate([first, second], axis=0)
            high = both.astype(BF16)
            taps_v[t * 16:(t + 1) * 16, lanes] = high
            taps_v[tokens + t * 16:tokens + (t + 1) * 16, lanes] = (both - high.astype(F32)).astype(BF16)
        return carry

    lax.fori_loop(0, blocks, filter_block, 0)

    for d in range(1, nx):
        src = lax.rem(mx + d, nx)
        pltpu.make_async_remote_copy(
            src_ref=sq_v.at[src], dst_ref=sq_v.at[src], send_sem=sq_send.at[d], recv_sem=sq_recv.at[src],
            device_id={"ch": src}, device_id_type=MESH).wait_recv()
    squares = jnp.sum(total_of([sq_v[i] for i in range(nx)]), axis=0, keepdims=True)
    scale = lax.rsqrt(squares / (nx * chans) + EPS)
    scol_v[...] = jnp.broadcast_to(scale, (tokens, LANES)).T

    def state_copy(b):
        return pltpu.make_async_remote_copy(
            src_ref=st_out.at[b], dst_ref=st_in.at[mj], send_sem=st_send.at[b], recv_sem=st_recv.at[mj],
            device_id=group_peer(b), device_id_type=MESH)

    def state_block(i, carry):
        b = lax.rem(mj + spread(i), nj)
        lanes = pl.ds(pl.multiple_of(b * LANES, LANES), LANES)
        jump = rows_of(jump_v[:, lanes])
        gain = gain_v[pl.ds(b, 1), :]
        sums = [None] * modes
        for t in range(tokens // 16):
            value = x_v[t * 16:(t + 1) * 16, lanes].astype(F32) * scol_v[t * 16:(t + 1) * 16, :] * gain
            value = value.astype(BF16)
            xn_v[t * 16:(t + 1) * 16, lanes] = value
            value = value.astype(F32)
            for part in (value[:8], value[8:]):
                sums = [part if s is None else s * c + part for s, c in zip(sums, jump)]
        sums = [s * left_v[b * modes + m] for m, s in enumerate(sums)]
        sums = jnp.concatenate([row_sums(sums[n:n + 8]) for n in range(0, modes, 8)], axis=0)
        st_out[b] = sums.astype(st_out.dtype)

        @pl.when(late & (i < nj - 1))
        def _():
            state_copy(b).start()

        return carry

    lax.fori_loop(0, nj, state_block, 0)
    st_in[mj] = st_out[mj]

    @pl.when(jnp.logical_not(late))
    def _():
        pl.semaphore_wait(barrier, nj // 2)

        def send_state(i, carry):
            state_copy(lax.rem(mj + spread(i), nj)).start()
            return carry

        lax.fori_loop(0, nj - 1, send_state, 0)

    def local_conv(c, carry):
        lanes = pl.ds(pl.multiple_of(c * width, width), width)
        xn = xn_v[:, lanes]
        high = taps_v[:tokens, lanes]
        low = taps_v[tokens:, lanes]
        spec = jnp.dot(fwd_v[...], jnp.concatenate([xn, xn], axis=0), preferred_element_type=F32)
        filt = jnp.dot(fwd_v[...], jnp.concatenate([high, high], axis=0), preferred_element_type=F32)
        filt = filt + jnp.dot(fwd_v[:, :tokens], low, preferred_element_type=F32)
        xr, xi = spec[:tokens], spec[tokens:]
        fr, fi = filt[:tokens], filt[tokens:]
        prod = jnp.concatenate([xr * fr - xi * fi, xr * fi + xi * fr], axis=0)
        phigh = prod.astype(BF16)
        plow = (prod - phigh.astype(F32)).astype(BF16)
        conv = jnp.dot(inv_v[...], jnp.concatenate([phigh, phigh], axis=0), preferred_element_type=F32)
        conv = conv + jnp.dot(inv_v[:, :2 * tokens], plow, preferred_element_type=F32)
        per = width // LANES
        skip = jnp.concatenate([skip_v[pl.ds(c * per + n, 1), :] for n in range(per)], axis=1)
        conv_v[:, lanes] = conv + skip * xn.astype(F32)
        return carry

    chunks = chans // width
    cut1, cut2 = chunks // 2, (3 * chunks) // 4
    lax.fori_loop(0, cut1, local_conv, 0)

    own = pl.ds(pl.multiple_of(mj * LANES, LANES), LANES)
    rate = rate_v[:, own]
    decay = jnp.exp(-float(tokens) * rate)

    def scan_group(k, state):
        @pl.when(k != mj)
        def _():
            pltpu.make_async_remote_copy(
                src_ref=st_out.at[k], dst_ref=st_in.at[k], send_sem=st_send.at[k], recv_sem=st_recv.at[k],
                device_id=group_peer(k), device_id_type=MESH).wait_recv()

        pre_v[k] = state
        return state * decay + st_in[k].astype(F32)

    tot_v[my] = lax.fori_loop(0, nj, scan_group, jnp.zeros((modes, LANES), F32))

    tot_copies = []
    for d in range(1, ny):
        copy = pltpu.make_async_remote_copy(
            src_ref=tot_v.at[my], dst_ref=tot_v.at[my], send_sem=tot_send.at[d], recv_sem=tot_recv.at[my],
            device_id={"seq": lax.rem(seq + d * nj, ny * nj)}, device_id_type=MESH)
        copy.start()
        tot_copies.append(copy)

    lax.fori_loop(cut1, cut2, local_conv, 0)

    for d in range(1, ny):
        src = lax.rem(my + d, ny)
        pltpu.make_async_remote_copy(
            src_ref=tot_v.at[src], dst_ref=tot_v.at[src], send_sem=tot_send.at[d], recv_sem=tot_recv.at[src],
            device_id={"seq": src * nj + mj}, device_id_type=MESH).wait_recv()
    before = jnp.zeros((modes, LANES), F32)
    for k in range(ny):
        steps = jnp.maximum(my - 1 - k, 0) * (nj * tokens)
        live = (k < my).astype(F32)
        before = before + live * jnp.exp(-rate * steps.astype(F32)) * tot_v[k]
    scaled = res_v[:, own] * jnp.sqrt(one_minus_exp_neg(2.0 * rate)) * jnp.exp(-rate)

    def carry_copy(k):
        return pltpu.make_async_remote_copy(
            src_ref=ca_out.at[k], dst_ref=ca_in.at[mj], send_sem=ca_send.at[k], recv_sem=ca_recv.at[mj],
            device_id=group_peer(k), device_id_type=MESH)

    def send_carry(i, carry):
        k = lax.rem(mj + spread(i), nj)
        past = pre_v[k] + jnp.exp(-rate * (k * tokens).astype(F32)) * before
        ca_out[k] = (scaled * past).astype(ca_out.dtype)

        @pl.when(i < nj - 1)
        def _():
            carry_copy(k).start()

        return carry

    lax.fori_loop(0, nj, send_carry, 0)
    ca_in[mj] = ca_out[mj]

    lax.fori_loop(cut2, chunks, local_conv, 0)
    staged[6].wait()

    def finish_block(i, carry):
        b = lax.rem(mj + 2 * nj - spread(nj - 1 - i), nj)

        @pl.when(b != mj)
        def _():
            pltpu.make_async_remote_copy(
                src_ref=ca_out.at[b], dst_ref=ca_in.at[b], send_sem=ca_send.at[b], recv_sem=ca_recv.at[b],
                device_id=group_peer(b), device_id_type=MESH).wait_recv()

        lanes = pl.ds(pl.multiple_of(b * LANES, LANES), LANES)
        jump = rows_of(jump_v[:, lanes])
        weight = ca_in[b].astype(F32)
        terms = [pow_v[b * modes + m] * weight[m:m + 1, :] for m in range(modes)]
        for t in range(tokens // 16):
            first = total_of(terms)
            terms = [a * c for a, c in zip(terms, jump)]
            second = total_of(terms)
            if t < tokens // 16 - 1:
                terms = [a * c for a, c in zip(terms, jump)]
            both = jnp.concatenate([first, second], axis=0) + conv_v[t * 16:(t + 1) * 16, lanes]
            gate = gate_v[t * 16:(t + 1) * 16, lanes].astype(F32)
            out_ref[t * 16:(t + 1) * 16, lanes] = (both * gate).astype(BF16)
        return carry

    lax.fori_loop(0, blocks, finish_block, 0)

    for copy in sq_copies + tot_copies:
        copy.wait_send()

    def drain(k, carry):
        @pl.when(k != mj)
        def _():
            state_copy(k).wait_send()
            carry_copy(k).wait_send()

        return carry

    lax.fori_loop(0, nj, drain, 0)


def shards(nx, nseq, stream, norm_gain, gate_act, decay_rate, residue, skip_gain):
    tokens, chans = stream.shape
    modes = decay_rate.shape[1]
    blocks = chans // LANES
    nj = blocks
    ny = nseq // nj
    width = 256
    fwd, inv = half_tables(tokens)
    any_spec = pl.BlockSpec(memory_space=pl.ANY)
    vmem = pltpu.VMEM
    dma = pltpu.SemaphoreType.DMA
    return pl.pallas_call(
        functools.partial(kernel, nx, ny, nj, modes, width),
        out_shape=jax.ShapeDtypeStruct((tokens, chans), BF16),
        in_specs=[any_spec] * 8,
        out_specs=pl.BlockSpec(memory_space=pltpu.VMEM),
        scratch_shapes=[
            vmem((tokens, chans), BF16),
            vmem((tokens, chans), BF16),
            vmem((modes, chans), F32),
            vmem((modes, chans), F32),
            vmem((blocks, LANES), F32),
            vmem((blocks, LANES), F32),
            vmem(fwd.shape, BF16),
            vmem(inv.shape, BF16),
            vmem((tokens, LANES), F32),
            vmem((nx, 8, LANES), F32),
            vmem((tokens, LANES), F32),
            vmem((blocks * modes, 8, LANES), F32),
            vmem((2 * tokens, chans), BF16),
            vmem((tokens, chans), BF16),
            vmem((tokens, chans), F32),
            vmem((blocks * modes, 8, LANES), F32),
            vmem((modes, chans), F32),
            vmem((nj, modes, LANES), WIRE),
            vmem((nj, modes, LANES), WIRE),
            vmem((ny, modes, LANES), F32),
            vmem((nj, modes, LANES), F32),
            vmem((nj, modes, LANES), WIRE),
            vmem((nj, modes, LANES), WIRE),
            dma((7,)),
            dma((4,)),
            dma((nx,)),
            dma((nx,)),
            dma((nj,)),
            dma((nj,)),
            dma((ny,)),
            dma((ny,)),
            dma((nj,)),
            dma((nj,)),
        ],
        compiler_params=pltpu.CompilerParams(
            collective_id=0, has_side_effects=True, vmem_limit_bytes=40 * 1024 * 1024
        ),
    )(*[pltpu.with_memory_space_constraint(v, pltpu.HBM) for v in (
        stream,
        decay_rate.T,
        residue.T,
        norm_gain.reshape(blocks, LANES),
        skip_gain.reshape(blocks, LANES),
        gate_act,
        jnp.asarray(fwd),
        jnp.asarray(inv),
    )])


def solution(mesh):
    in_specs = (P("seq", "ch"), P("ch"), P("seq", "ch"), P("ch", None), P("ch", None), P("ch"))
    body = functools.partial(shards, mesh.shape["ch"], mesh.shape["seq"])
    return jax.shard_map(body, mesh=mesh, in_specs=in_specs, out_specs=P("seq", "ch"), check_vma=False)
```

```python
import functools
import math

import jax
import jax.numpy as jnp
import numpy as np
from jax import lax
from jax.experimental import pallas as pl
from jax.experimental.pallas import tpu as pltpu
from jax.sharding import PartitionSpec as P

MESH = pl.DeviceIdType.MESH
EPS = 1e-06
LANES = 128
WIRE = jnp.bfloat16
F32 = jnp.float32
BF16 = jnp.bfloat16


def half_tables(length):
    k = np.arange(length)[:, None] + 0.5
    t = np.arange(length)[None, :]
    angle = np.pi * k * t / length
    forward = np.concatenate([np.cos(angle), -np.sin(angle)], axis=0)
    inverse = np.concatenate([np.cos(angle.T), -np.sin(angle.T)], axis=1) / length

    def split(table):
        high = table.astype(BF16)
        low = (table - high.astype(np.float64)).astype(BF16)
        return np.concatenate([high, low], axis=1)

    return split(forward), split(inverse)


def one_minus_exp_neg(z):
    series = jnp.ones_like(z)
    for n in range(10, 1, -1):
        series = 1.0 - z * series * (1.0 / n)
    return jnp.where(z < 0.5, z * series, 1.0 - jnp.exp(-z))


def total_of(items):
    items = list(items)
    while len(items) > 1:
        items = [a + b for a, b in zip(items[::2], items[1::2])] + ([items[-1]] if len(items) % 2 else [])
    return items[0]


def rows_of(tile):
    return [jnp.broadcast_to(tile[m:m + 1, :], (8, LANES)) for m in range(tile.shape[0])]


def row_sums(tiles):
    row = lax.broadcasted_iota(jnp.int32, (8, LANES), 0)
    for bit in (4, 2, 1):
        clear = lax.rem(row // bit, 2) == 0
        count = len(tiles) // 2
        tiles = [jnp.where(clear, a + pltpu.roll(a, 8 - bit, 0), c + pltpu.roll(c, bit, 0))
                 for a, c in zip(tiles[:count], tiles[count:])]
    return tiles[0]


def kernel(nx, ny, nj, modes, width,
           x_hbm, rate_hbm, res_hbm, gain_hbm, skip_hbm, gate_hbm, fwd_hbm, inv_hbm, out_ref,
           x_v, gate_v, rate_v, res_v, gain_v, skip_v, fwd_v, inv_v,
           sqacc_v, sq_v, scol_v, pow_v, taps_v, conv_v, left_v, jump_v,
           st_out, st_in, tot_v, before_v, pre_v, fac_v, ca_out, ca_in,
           in_sem, x_sem, sq_send, sq_recv, st_send, st_recv, tot_send, tot_recv, ca_send, ca_recv):
    tokens, chans = x_v.shape
    blocks = chans // LANES
    mx = lax.axis_index("ch")
    seq = lax.axis_index("seq")
    my = seq // nj
    mj = lax.rem(seq, nj)

    def group_peer(k):
        return {"seq": my * nj + k}

    def spread(i):
        return nj // 2 + jnp.where(lax.rem(i, 2) == 1, (i + 1) // 2, -(i // 2))

    parts = x_sem.shape[0]
    rows_part = tokens // parts
    for p in range(parts):
        rows = pl.ds(p * rows_part, rows_part)
        pltpu.make_async_copy(x_hbm.at[rows], x_v.at[rows], x_sem.at[p]).start()
    staged = [(rate_hbm, rate_v), (res_hbm, res_v), (gain_hbm, gain_v), (skip_hbm, skip_v),
              (fwd_hbm, fwd_v), (inv_hbm, inv_v), (gate_hbm, gate_v)]
    staged = [pltpu.make_async_copy(a, b, in_sem.at[n]) for n, (a, b) in enumerate(staged)]
    for copy in staged:
        copy.start()

    half = nj // 2
    late = mj >= half
    barrier = pltpu.get_barrier_semaphore()
    for d in range(1, nx):
        pl.semaphore_signal(barrier, inc=1, device_id={"ch": lax.rem(mx + d, nx)}, device_id_type=MESH)
    for d in range(1, ny):
        pl.semaphore_signal(barrier, inc=1, device_id={"seq": lax.rem(seq + d * nj, ny * nj)}, device_id_type=MESH)

    def greet(first):
        for k in range(first, first + half):
            @pl.when(k != mj)
            def _():
                pl.semaphore_signal(barrier, inc=1, device_id=group_peer(k), device_id_type=MESH)

    @pl.when(late)
    def _():
        greet(half)

    tiles_part = rows_part // 16
    for p in range(parts):
        rows = pl.ds(p * rows_part, rows_part)
        pltpu.make_async_copy(x_hbm.at[rows], x_v.at[rows], x_sem.at[p]).wait()

        def square_rows(i, carry):
            part = pl.ds(pl.multiple_of(p * rows_part + i * 16, 16), 16)
            pieces = []
            for b in range(blocks):
                v = x_v[part, b * LANES:(b + 1) * LANES].astype(F32)
                pieces.append(v * v)
            sqacc_v[part, :] = total_of(pieces)
            return carry

        lax.fori_loop(0, tiles_part, square_rows, 0)
    turned = sqacc_v[...].T
    sq_v[mx] = total_of([turned[i * 8:(i + 1) * 8] for i in range(LANES // 8)])

    @pl.when(late)
    def _():
        pl.semaphore_wait(barrier, nx + ny + nj - 3)
        greet(0)

    @pl.when(jnp.logical_not(late))
    def _():
        pl.semaphore_wait(barrier, nx + ny - 2)
        greet(half)

    sq_copies = []
    for d in range(1, nx):
        copy = pltpu.make_async_remote_copy(
            src_ref=sq_v.at[mx], dst_ref=sq_v.at[mx], send_sem=sq_send.at[d], recv_sem=sq_recv.at[mx],
            device_id={"ch": lax.rem(mx + d, nx)}, device_id_type=MESH)
        copy.start()
        sq_copies.append(copy)

    for copy in staged[:6]:
        copy.wait()
    step8 = lax.broadcasted_iota(jnp.int32, (8, LANES), 0).astype(F32)

    def filter_block(b, carry):
        lanes = pl.ds(pl.multiple_of(b * LANES, LANES), LANES)
        rate = rate_v[:, lanes]
        weight = res_v[:, lanes] * jnp.sqrt(one_minus_exp_neg(2.0 * rate))
        jump = jnp.exp(-8.0 * rate)
        jump_v[:, lanes] = jump
        jump = rows_of(jump)
        terms = []
        for m in range(modes):
            power = jnp.exp(-rate[m:m + 1, :] * step8)
            pow_v[b * modes + m] = power
            left_v[b * modes + m] = jnp.exp(-rate[m:m + 1, :] * (7.0 - step8))
            terms.append(power * weight[m:m + 1, :])
        for t in range(tokens // 16):
            first = total_of(terms)
            terms = [a * c for a, c in zip(terms, jump)]
            second = total_of(terms)
            if t < tokens // 16 - 1:
                terms = [a * c for a, c in zip(terms, jump)]
            both = jnp.concatenate([first, second], axis=0)
            high = both.astype(BF16)
            taps_v[t * 16:(t + 1) * 16, lanes] = high
            taps_v[tokens + t * 16:tokens + (t + 1) * 16, lanes] = (both - high.astype(F32)).astype(BF16)
        return carry

    lax.fori_loop(0, blocks, filter_block, 0)

    for d in range(1, nx):
        src = lax.rem(mx + d, nx)
        pltpu.make_async_remote_copy(
            src_ref=sq_v.at[src], dst_ref=sq_v.at[src], send_sem=sq_send.at[d], recv_sem=sq_recv.at[src],
            device_id={"ch": src}, device_id_type=MESH).wait_recv()
    squares = jnp.sum(total_of([sq_v[i] for i in range(nx)]), axis=0, keepdims=True)
    scale = lax.rsqrt(squares / (nx * chans) + EPS)
    scol_v[...] = jnp.broadcast_to(scale, (tokens, LANES)).T

    def state_copy(b):
        return pltpu.make_async_remote_copy(
            src_ref=st_out.at[b], dst_ref=st_in.at[mj], send_sem=st_send.at[b], recv_sem=st_recv.at[mj],
            device_id=group_peer(b), device_id_type=MESH)

    def state_of(b):
        lanes = pl.ds(pl.multiple_of(b * LANES, LANES), LANES)
        jump = rows_of(jump_v[:, lanes])
        sums = [None] * modes
        for t in range(tokens // 16):
            value = x_v[t * 16:(t + 1) * 16, lanes].astype(F32) * scol_v[t * 16:(t + 1) * 16, :]
            for part in (value[:8], value[8:]):
                sums = [part if s is None else s * c + part for s, c in zip(sums, jump)]
        sums = [s * left_v[b * modes + m] for m, s in enumerate(sums)]
        sums = jnp.concatenate([row_sums(sums[n:n + 8]) for n in range(0, modes, 8)], axis=0)
        st_out[b] = (sums * gain_v[pl.ds(b, 1), :]).astype(st_out.dtype)

    def state_blocks(i, carry):
        pair = [lax.rem(mj + spread(2 * i + n), nj) for n in range(2)]
        for b in pair:
            state_of(b)

        @pl.when(late)
        def _():
            state_copy(pair[0]).start()

            @pl.when(i < nj // 2 - 1)
            def _():
                state_copy(pair[1]).start()

        return carry

    lax.fori_loop(0, nj // 2, state_blocks, 0)
    st_in[mj] = st_out[mj]

    @pl.when(jnp.logical_not(late))
    def _():
        pl.semaphore_wait(barrier, nj // 2)

        def send_state(i, carry):
            state_copy(lax.rem(mj + spread(i), nj)).start()
            return carry

        lax.fori_loop(0, nj - 1, send_state, 0)

    def local_conv(c, carry):
        lanes = pl.ds(pl.multiple_of(c * width, width), width)
        per = width // LANES
        scale = jnp.concatenate([scol_v[...]] * per, axis=1)
        gain = jnp.concatenate([gain_v[pl.ds(c * per + n, 1), :] for n in range(per)], axis=1)
        xn = (x_v[:, lanes].astype(F32) * scale * gain).astype(BF16)
        high = taps_v[:tokens, lanes]
        low = taps_v[tokens:, lanes]
        spec = jnp.dot(fwd_v[...], jnp.concatenate([xn, xn], axis=0), preferred_element_type=F32)
        filt = jnp.dot(fwd_v[...], jnp.concatenate([high, high], axis=0), preferred_element_type=F32)
        filt = filt + jnp.dot(fwd_v[:, :tokens], low, preferred_element_type=F32)
        xr, xi = spec[:tokens], spec[tokens:]
        fr, fi = filt[:tokens], filt[tokens:]
        prod = jnp.concatenate([xr * fr - xi * fi, xr * fi + xi * fr], axis=0)
        phigh = prod.astype(BF16)
        plow = (prod - phigh.astype(F32)).astype(BF16)
        conv = jnp.dot(inv_v[...], jnp.concatenate([phigh, phigh], axis=0), preferred_element_type=F32)
        conv = conv + jnp.dot(inv_v[:, :2 * tokens], plow, preferred_element_type=F32)
        skip = jnp.concatenate([skip_v[pl.ds(c * per + n, 1), :] for n in range(per)], axis=1)
        conv_v[:, lanes] = conv + skip * xn.astype(F32)
        return carry

    chunks = chans // width
    cut1, cut2 = chunks // 2, (3 * chunks) // 4
    lax.fori_loop(0, cut1, local_conv, 0)

    own = pl.ds(pl.multiple_of(mj * LANES, LANES), LANES)
    rate = rate_v[:, own]
    decay = jnp.exp(-float(tokens) * rate)

    def scan_group(k, state):
        @pl.when(k != mj)
        def _():
            pltpu.make_async_remote_copy(
                src_ref=st_out.at[k], dst_ref=st_in.at[k], send_sem=st_send.at[k], recv_sem=st_recv.at[k],
                device_id=group_peer(k), device_id_type=MESH).wait_recv()

        pre_v[k] = state
        return state * decay + st_in[k].astype(F32)

    tot_v[my] = lax.fori_loop(0, nj, scan_group, jnp.zeros((modes, LANES), F32))

    def total_copy(d):
        return pltpu.make_async_remote_copy(
            src_ref=tot_v.at[my], dst_ref=tot_v.at[my], send_sem=tot_send.at[d], recv_sem=tot_recv.at[my],
            device_id={"seq": lax.rem(seq + d * nj, ny * nj)}, device_id_type=MESH)

    for d in range(1, ny):
        @pl.when(my + d < ny)
        def _():
            total_copy(d).start()

    lax.fori_loop(cut1, cut2, local_conv, 0)

    scaled = res_v[:, own] * jnp.sqrt(one_minus_exp_neg(2.0 * rate)) * jnp.exp(-rate)
    shares = []
    for k in range(ny - 1):
        steps = jnp.maximum(my - 1 - k, 0) * (nj * tokens)
        shares.append(jnp.exp(-rate * steps.astype(F32)))

    def factors(k, carry):
        pre_v[k] = scaled * pre_v[k]
        fac_v[k] = scaled * jnp.exp(-rate * (k * tokens).astype(F32))
        return carry

    lax.fori_loop(0, nj, factors, 0)
    before_v[...] = jnp.zeros((modes, LANES), F32)
    for k in range(ny - 1):
        @pl.when(k < my)
        def _():
            pltpu.make_async_remote_copy(
                src_ref=tot_v.at[k], dst_ref=tot_v.at[k], send_sem=tot_send.at[1], recv_sem=tot_recv.at[k],
                device_id={"seq": k * nj + mj}, device_id_type=MESH).wait_recv()
            before_v[...] += shares[k] * tot_v[k]

    before = before_v[...]

    def carry_copy(k):
        return pltpu.make_async_remote_copy(
            src_ref=ca_out.at[k], dst_ref=ca_in.at[mj], send_sem=ca_send.at[k], recv_sem=ca_recv.at[mj],
            device_id=group_peer(k), device_id_type=MESH)

    def send_carry(i, carry):
        k = lax.rem(mj + spread(i), nj)
        ca_out[k] = (pre_v[k] + fac_v[k] * before).astype(ca_out.dtype)

        @pl.when(i < nj - 1)
        def _():
            carry_copy(k).start()

        return carry

    lax.fori_loop(0, nj, send_carry, 0)
    ca_in[mj] = ca_out[mj]

    lax.fori_loop(cut2, chunks, local_conv, 0)
    staged[6].wait()
    for copy in sq_copies:
        copy.wait_send()
    for d in range(1, ny):
        @pl.when(my + d < ny)
        def _():
            total_copy(d).wait_send()

    def drain_states(k, carry):
        @pl.when(k != mj)
        def _():
            state_copy(k).wait_send()

        return carry

    lax.fori_loop(0, nj, drain_states, 0)

    def finish_block(i, carry):
        b = lax.rem(mj + 2 * nj - spread(nj - 1 - i), nj)

        @pl.when(b != mj)
        def _():
            pltpu.make_async_remote_copy(
                src_ref=ca_out.at[b], dst_ref=ca_in.at[b], send_sem=ca_send.at[b], recv_sem=ca_recv.at[b],
                device_id=group_peer(b), device_id_type=MESH).wait_recv()

        lanes = pl.ds(pl.multiple_of(b * LANES, LANES), LANES)
        jump = rows_of(jump_v[:, lanes])
        weight = ca_in[b].astype(F32)
        terms = [pow_v[b * modes + m] * weight[m:m + 1, :] for m in range(modes)]
        for t in range(tokens // 16):
            first = total_of(terms)
            terms = [a * c for a, c in zip(terms, jump)]
            second = total_of(terms)
            if t < tokens // 16 - 1:
                terms = [a * c for a, c in zip(terms, jump)]
            both = jnp.concatenate([first, second], axis=0) + conv_v[t * 16:(t + 1) * 16, lanes]
            gate = gate_v[t * 16:(t + 1) * 16, lanes].astype(F32)
            out_ref[t * 16:(t + 1) * 16, lanes] = (both * gate).astype(BF16)
        return carry

    def drain_carries(k, carry):
        @pl.when(k != mj)
        def _():
            carry_copy(k).wait_send()

        return carry

    lax.fori_loop(0, blocks // 4, finish_block, 0)
    lax.fori_loop(0, nj, drain_carries, 0)
    lax.fori_loop(blocks // 4, blocks, finish_block, 0)


def shards(nx, nseq, stream, norm_gain, gate_act, decay_rate, residue, skip_gain):
    tokens, chans = stream.shape
    modes = decay_rate.shape[1]
    blocks = chans // LANES
    nj = blocks
    ny = nseq // nj
    width = 256
    fwd, inv = half_tables(tokens)
    any_spec = pl.BlockSpec(memory_space=pl.ANY)
    vmem = pltpu.VMEM
    dma = pltpu.SemaphoreType.DMA
    return pl.pallas_call(
        functools.partial(kernel, nx, ny, nj, modes, width),
        out_shape=jax.ShapeDtypeStruct((tokens, chans), BF16),
        in_specs=[any_spec] * 8,
        out_specs=pl.BlockSpec(memory_space=pltpu.VMEM),
        scratch_shapes=[
            vmem((tokens, chans), BF16),
            vmem((tokens, chans), BF16),
            vmem((modes, chans), F32),
            vmem((modes, chans), F32),
            vmem((blocks, LANES), F32),
            vmem((blocks, LANES), F32),
            vmem(fwd.shape, BF16),
            vmem(inv.shape, BF16),
            vmem((tokens, LANES), F32),
            vmem((nx, 8, LANES), F32),
            vmem((tokens, LANES), F32),
            vmem((blocks * modes, 8, LANES), F32),
            vmem((2 * tokens, chans), BF16),
            vmem((tokens, chans), F32),
            vmem((blocks * modes, 8, LANES), F32),
            vmem((modes, chans), F32),
            vmem((nj, modes, LANES), WIRE),
            vmem((nj, modes, LANES), WIRE),
            vmem((ny, modes, LANES), F32),
            vmem((modes, LANES), F32),
            vmem((nj, modes, LANES), F32),
            vmem((nj, modes, LANES), F32),
            vmem((nj, modes, LANES), WIRE),
            vmem((nj, modes, LANES), WIRE),
            dma((7,)),
            dma((4,)),
            dma((nx,)),
            dma((nx,)),
            dma((nj,)),
            dma((nj,)),
            dma((ny,)),
            dma((ny,)),
            dma((nj,)),
            dma((nj,)),
        ],
        compiler_params=pltpu.CompilerParams(
            collective_id=0, has_side_effects=True, vmem_limit_bytes=40 * 1024 * 1024
        ),
    )(*[pltpu.with_memory_space_constraint(v, pltpu.HBM) for v in (
        stream,
        decay_rate.T,
        residue.T,
        norm_gain.reshape(blocks, LANES),
        skip_gain.reshape(blocks, LANES),
        gate_act,
        jnp.asarray(fwd),
        jnp.asarray(inv),
    )])


def solution(mesh):
    in_specs = (P("seq", "ch"), P("ch"), P("seq", "ch"), P("ch", None), P("ch", None), P("ch"))
    body = functools.partial(shards, mesh.shape["ch"], mesh.shape["seq"])
    return jax.shard_map(body, mesh=mesh, in_specs=in_specs, out_specs=P("seq", "ch"), check_vma=False)
```

```python
import functools
import math

import jax
import jax.numpy as jnp
import numpy as np
from jax import lax
from jax.experimental import pallas as pl
from jax.experimental.pallas import tpu as pltpu
from jax.sharding import PartitionSpec as P

MESH = pl.DeviceIdType.MESH
EPS = 1e-06
LANES = 128
WIRE = jnp.bfloat16
F32 = jnp.float32
BF16 = jnp.bfloat16


def half_tables(length):
    k = np.arange(length)[:, None] + 0.5
    t = np.arange(length)[None, :]
    angle = np.pi * k * t / length
    forward = np.concatenate([np.cos(angle), -np.sin(angle)], axis=0)
    inverse = np.concatenate([np.cos(angle.T), -np.sin(angle.T)], axis=1) / length

    def split(table):
        high = table.astype(BF16)
        low = (table - high.astype(np.float64)).astype(BF16)
        return np.concatenate([high, low], axis=1)

    return split(forward), split(inverse)


def one_minus_exp_neg(z):
    series = jnp.ones_like(z)
    for n in range(10, 1, -1):
        series = 1.0 - z * series * (1.0 / n)
    return jnp.where(z < 0.5, z * series, 1.0 - jnp.exp(-z))


def total_of(items):
    items = list(items)
    while len(items) > 1:
        items = [a + b for a, b in zip(items[::2], items[1::2])] + ([items[-1]] if len(items) % 2 else [])
    return items[0]


def rows_of(tile):
    return [jnp.broadcast_to(tile[m:m + 1, :], (8, LANES)) for m in range(tile.shape[0])]


def row_sums(tiles):
    row = lax.broadcasted_iota(jnp.int32, (8, LANES), 0)
    for bit in (4, 2, 1):
        clear = lax.rem(row // bit, 2) == 0
        count = len(tiles) // 2
        tiles = [jnp.where(clear, a + pltpu.roll(a, 8 - bit, 0), c + pltpu.roll(c, bit, 0))
                 for a, c in zip(tiles[:count], tiles[count:])]
    return tiles[0]


def kernel(nx, ny, nj, modes, width,
           x_hbm, rate_hbm, res_hbm, gain_hbm, skip_hbm, gate_hbm, fwd_hbm, inv_hbm, out_ref,
           x_v, gate_v, rate_v, res_v, gain_v, skip_v, fwd_v, inv_v,
           sqacc_v, sq_v, scol_v, pow_v, taps_v, conv_v, left_v, jump_v,
           st_out, st_in, tot_v, before_v, pre_v, fac_v, ca_out, ca_in,
           in_sem, x_sem, sq_send, sq_recv, st_send, st_recv, tot_send, tot_recv, ca_send, ca_recv):
    tokens, chans = x_v.shape
    blocks = chans // LANES
    mx = lax.axis_index("ch")
    seq = lax.axis_index("seq")
    my = seq // nj
    mj = lax.rem(seq, nj)

    def group_peer(k):
        return {"seq": my * nj + k}

    def spread(i):
        return nj // 2 + jnp.where(lax.rem(i, 2) == 1, (i + 1) // 2, -(i // 2))

    parts = x_sem.shape[0]
    rows_part = tokens // parts
    for p in range(parts):
        rows = pl.ds(p * rows_part, rows_part)
        pltpu.make_async_copy(x_hbm.at[rows], x_v.at[rows], x_sem.at[p]).start()
    staged = [(rate_hbm, rate_v), (res_hbm, res_v), (gain_hbm, gain_v), (skip_hbm, skip_v),
              (fwd_hbm, fwd_v), (inv_hbm, inv_v), (gate_hbm, gate_v)]
    staged = [pltpu.make_async_copy(a, b, in_sem.at[n]) for n, (a, b) in enumerate(staged)]
    for copy in staged:
        copy.start()

    half = nj // 2
    late = mj >= half
    barrier = pltpu.get_barrier_semaphore()
    for d in range(1, nx):
        pl.semaphore_signal(barrier, inc=1, device_id={"ch": lax.rem(mx + d, nx)}, device_id_type=MESH)
    for d in range(1, ny):
        pl.semaphore_signal(barrier, inc=1, device_id={"seq": lax.rem(seq + d * nj, ny * nj)}, device_id_type=MESH)

    def greet(first):
        for k in range(first, first + half):
            @pl.when(k != mj)
            def _():
                pl.semaphore_signal(barrier, inc=1, device_id=group_peer(k), device_id_type=MESH)

    @pl.when(late)
    def _():
        greet(half)

    tiles_part = rows_part // 16
    for p in range(parts):
        rows = pl.ds(p * rows_part, rows_part)
        pltpu.make_async_copy(x_hbm.at[rows], x_v.at[rows], x_sem.at[p]).wait()

        def square_rows(i, carry):
            part = pl.ds(pl.multiple_of(p * rows_part + i * 16, 16), 16)
            pieces = []
            for b in range(blocks):
                v = x_v[part, b * LANES:(b + 1) * LANES].astype(F32)
                pieces.append(v * v)
            sqacc_v[part, :] = total_of(pieces)
            return carry

        lax.fori_loop(0, tiles_part, square_rows, 0)
    turned = sqacc_v[...].T
    sq_v[mx] = total_of([turned[i * 8:(i + 1) * 8] for i in range(LANES // 8)])

    @pl.when(late)
    def _():
        pl.semaphore_wait(barrier, nx + ny + nj - 3)
        greet(0)

    @pl.when(jnp.logical_not(late))
    def _():
        pl.semaphore_wait(barrier, nx + ny - 2)
        greet(half)

    sq_copies = []
    for d in range(1, nx):
        copy = pltpu.make_async_remote_copy(
            src_ref=sq_v.at[mx], dst_ref=sq_v.at[mx], send_sem=sq_send.at[d], recv_sem=sq_recv.at[mx],
            device_id={"ch": lax.rem(mx + d, nx)}, device_id_type=MESH)
        copy.start()
        sq_copies.append(copy)

    for copy in staged[:6]:
        copy.wait()
    step8 = lax.broadcasted_iota(jnp.int32, (8, LANES), 0).astype(F32)

    def filter_block(b, carry):
        lanes = pl.ds(pl.multiple_of(b * LANES, LANES), LANES)
        rate = rate_v[:, lanes]
        weight = res_v[:, lanes] * jnp.sqrt(one_minus_exp_neg(2.0 * rate))
        jump = jnp.exp(-8.0 * rate)
        jump_v[:, lanes] = jump
        jump = rows_of(jump)
        terms = []
        for m in range(modes):
            power = jnp.exp(-rate[m:m + 1, :] * step8)
            pow_v[b * modes + m] = power
            left_v[b * modes + m] = jnp.exp(-rate[m:m + 1, :] * (7.0 - step8))
            terms.append(power * weight[m:m + 1, :])
        for t in range(tokens // 16):
            first = total_of(terms)
            terms = [a * c for a, c in zip(terms, jump)]
            second = total_of(terms)
            if t < tokens // 16 - 1:
                terms = [a * c for a, c in zip(terms, jump)]
            both = jnp.concatenate([first, second], axis=0)
            taps_v[t * 16:(t + 1) * 16, lanes] = both.astype(BF16)
        return carry

    lax.fori_loop(0, blocks, filter_block, 0)

    for d in range(1, nx):
        src = lax.rem(mx + d, nx)
        pltpu.make_async_remote_copy(
            src_ref=sq_v.at[src], dst_ref=sq_v.at[src], send_sem=sq_send.at[d], recv_sem=sq_recv.at[src],
            device_id={"ch": src}, device_id_type=MESH).wait_recv()
    squares = jnp.sum(total_of([sq_v[i] for i in range(nx)]), axis=0, keepdims=True)
    scale = lax.rsqrt(squares / (nx * chans) + EPS)
    scol_v[...] = jnp.broadcast_to(scale, (tokens, LANES)).T

    def state_copy(b):
        return pltpu.make_async_remote_copy(
            src_ref=st_out.at[b], dst_ref=st_in.at[mj], send_sem=st_send.at[b], recv_sem=st_recv.at[mj],
            device_id=group_peer(b), device_id_type=MESH)

    def state_of(b):
        lanes = pl.ds(pl.multiple_of(b * LANES, LANES), LANES)
        jump = rows_of(jump_v[:, lanes])
        sums = [None] * modes
        for t in range(tokens // 16):
            value = x_v[t * 16:(t + 1) * 16, lanes].astype(F32) * scol_v[t * 16:(t + 1) * 16, :]
            for part in (value[:8], value[8:]):
                sums = [part if s is None else s * c + part for s, c in zip(sums, jump)]
        sums = [s * left_v[b * modes + m] for m, s in enumerate(sums)]
        sums = jnp.concatenate([row_sums(sums[n:n + 8]) for n in range(0, modes, 8)], axis=0)
        st_out[b] = (sums * gain_v[pl.ds(b, 1), :]).astype(st_out.dtype)

    def state_blocks(i, carry):
        pair = [lax.rem(mj + spread(2 * i + n), nj) for n in range(2)]
        for b in pair:
            state_of(b)

        @pl.when(late)
        def _():
            state_copy(pair[0]).start()

            @pl.when(i < nj // 2 - 1)
            def _():
                state_copy(pair[1]).start()

        return carry

    lax.fori_loop(0, nj // 2, state_blocks, 0)
    st_in[mj] = st_out[mj]

    @pl.when(jnp.logical_not(late))
    def _():
        pl.semaphore_wait(barrier, nj // 2)

        def send_state(i, carry):
            state_copy(lax.rem(mj + spread(i), nj)).start()
            return carry

        lax.fori_loop(0, nj - 1, send_state, 0)

    def local_conv(c, carry):
        lanes = pl.ds(pl.multiple_of(c * width, width), width)
        per = width // LANES
        scale = jnp.concatenate([scol_v[...]] * per, axis=1)
        gain = jnp.concatenate([gain_v[pl.ds(c * per + n, 1), :] for n in range(per)], axis=1)
        xn = (x_v[:, lanes].astype(F32) * scale * gain).astype(BF16)
        taps = taps_v[:, lanes]
        spec = jnp.dot(fwd_v[...], jnp.concatenate([xn, xn], axis=0), preferred_element_type=F32)
        filt = jnp.dot(fwd_v[...], jnp.concatenate([taps, taps], axis=0), preferred_element_type=F32)
        xr, xi = spec[:tokens], spec[tokens:]
        fr, fi = filt[:tokens], filt[tokens:]
        prod = jnp.concatenate([xr * fr - xi * fi, xr * fi + xi * fr], axis=0)
        prod = prod.astype(BF16)
        conv = jnp.dot(inv_v[...], jnp.concatenate([prod, prod], axis=0), preferred_element_type=F32)
        skip = jnp.concatenate([skip_v[pl.ds(c * per + n, 1), :] for n in range(per)], axis=1)
        conv_v[:, lanes] = conv + skip * xn.astype(F32)
        return carry

    chunks = chans // width
    cut1, cut2 = (3 * chunks) // 8, (5 * chunks) // 8
    lax.fori_loop(0, cut1, local_conv, 0)

    own = pl.ds(pl.multiple_of(mj * LANES, LANES), LANES)
    rate = rate_v[:, own]
    decay = jnp.exp(-float(tokens) * rate)

    def scan_group(k, state):
        @pl.when(k != mj)
        def _():
            pltpu.make_async_remote_copy(
                src_ref=st_out.at[k], dst_ref=st_in.at[k], send_sem=st_send.at[k], recv_sem=st_recv.at[k],
                device_id=group_peer(k), device_id_type=MESH).wait_recv()

        pre_v[k] = state
        return state * decay + st_in[k].astype(F32)

    tot_v[my] = lax.fori_loop(0, nj, scan_group, jnp.zeros((modes, LANES), F32))

    def total_copy(d):
        return pltpu.make_async_remote_copy(
            src_ref=tot_v.at[my], dst_ref=tot_v.at[my], send_sem=tot_send.at[d], recv_sem=tot_recv.at[my],
            device_id={"seq": lax.rem(seq + d * nj, ny * nj)}, device_id_type=MESH)

    for d in range(1, ny):
        @pl.when(my + d < ny)
        def _():
            total_copy(d).start()

    lax.fori_loop(cut1, cut2, local_conv, 0)

    scaled = res_v[:, own] * jnp.sqrt(one_minus_exp_neg(2.0 * rate)) * jnp.exp(-rate)
    shares = []
    for k in range(ny - 1):
        steps = jnp.maximum(my - 1 - k, 0) * (nj * tokens)
        shares.append(jnp.exp(-rate * steps.astype(F32)))

    def factors(k, carry):
        pre_v[k] = scaled * pre_v[k]
        fac_v[k] = scaled * jnp.exp(-rate * (k * tokens).astype(F32))
        return carry

    lax.fori_loop(0, nj, factors, 0)
    before_v[...] = jnp.zeros((modes, LANES), F32)
    for k in range(ny - 1):
        @pl.when(k < my)
        def _():
            pltpu.make_async_remote_copy(
                src_ref=tot_v.at[k], dst_ref=tot_v.at[k], send_sem=tot_send.at[1], recv_sem=tot_recv.at[k],
                device_id={"seq": k * nj + mj}, device_id_type=MESH).wait_recv()
            before_v[...] += shares[k] * tot_v[k]

    before = before_v[...]

    def carry_copy(k):
        return pltpu.make_async_remote_copy(
            src_ref=ca_out.at[k], dst_ref=ca_in.at[mj], send_sem=ca_send.at[k], recv_sem=ca_recv.at[mj],
            device_id=group_peer(k), device_id_type=MESH)

    def send_carry(i, carry):
        k = lax.rem(mj + spread(i), nj)
        ca_out[k] = (pre_v[k] + fac_v[k] * before).astype(ca_out.dtype)

        @pl.when(i < nj - 1)
        def _():
            carry_copy(k).start()

        return carry

    lax.fori_loop(0, nj, send_carry, 0)
    ca_in[mj] = ca_out[mj]

    lax.fori_loop(cut2, chunks, local_conv, 0)
    staged[6].wait()
    for copy in sq_copies:
        copy.wait_send()
    for d in range(1, ny):
        @pl.when(my + d < ny)
        def _():
            total_copy(d).wait_send()

    def drain_states(k, carry):
        @pl.when(k != mj)
        def _():
            state_copy(k).wait_send()

        return carry

    lax.fori_loop(0, nj, drain_states, 0)

    def await_block(b):

        @pl.when(b != mj)
        def _():
            pltpu.make_async_remote_copy(
                src_ref=ca_out.at[b], dst_ref=ca_in.at[b], send_sem=ca_send.at[b], recv_sem=ca_recv.at[b],
                device_id=group_peer(b), device_id_type=MESH).wait_recv()

    def finish(b):
        lanes = pl.ds(pl.multiple_of(b * LANES, LANES), LANES)
        jump = rows_of(jump_v[:, lanes])
        weight = ca_in[b].astype(F32)
        terms = [pow_v[b * modes + m] * weight[m:m + 1, :] for m in range(modes)]
        for t in range(tokens // 16):
            first = total_of(terms)
            terms = [a * c for a, c in zip(terms, jump)]
            second = total_of(terms)
            if t < tokens // 16 - 1:
                terms = [a * c for a, c in zip(terms, jump)]
            both = jnp.concatenate([first, second], axis=0) + conv_v[t * 16:(t + 1) * 16, lanes]
            gate = gate_v[t * 16:(t + 1) * 16, lanes].astype(F32)
            out_ref[t * 16:(t + 1) * 16, lanes] = (both * gate).astype(BF16)

    def finish_blocks(i, carry):
        pair = [lax.rem(mj + 2 * nj - spread(nj - 1 - 2 * i - n), nj) for n in range(2)]
        for b in pair:
            await_block(b)
        for b in pair:
            finish(b)
        return carry

    def drain_carries(k, carry):
        @pl.when(k != mj)
        def _():
            carry_copy(k).wait_send()

        return carry

    lax.fori_loop(0, blocks // 8, finish_blocks, 0)
    lax.fori_loop(0, nj, drain_carries, 0)
    lax.fori_loop(blocks // 8, blocks // 2, finish_blocks, 0)


def shards(nx, nseq, stream, norm_gain, gate_act, decay_rate, residue, skip_gain):
    tokens, chans = stream.shape
    modes = decay_rate.shape[1]
    blocks = chans // LANES
    nj = blocks
    ny = nseq // nj
    width = 256
    fwd, inv = half_tables(tokens)
    any_spec = pl.BlockSpec(memory_space=pl.ANY)
    vmem = pltpu.VMEM
    dma = pltpu.SemaphoreType.DMA
    return pl.pallas_call(
        functools.partial(kernel, nx, ny, nj, modes, width),
        out_shape=jax.ShapeDtypeStruct((tokens, chans), BF16),
        in_specs=[any_spec] * 8,
        out_specs=pl.BlockSpec(memory_space=pltpu.VMEM),
        scratch_shapes=[
            vmem((tokens, chans), BF16),
            vmem((tokens, chans), BF16),
            vmem((modes, chans), F32),
            vmem((modes, chans), F32),
            vmem((blocks, LANES), F32),
            vmem((blocks, LANES), F32),
            vmem(fwd.shape, BF16),
            vmem(inv.shape, BF16),
            vmem((tokens, LANES), F32),
            vmem((nx, 8, LANES), F32),
            vmem((tokens, LANES), F32),
            vmem((blocks * modes, 8, LANES), F32),
            vmem((tokens, chans), BF16),
            vmem((tokens, chans), F32),
            vmem((blocks * modes, 8, LANES), F32),
            vmem((modes, chans), F32),
            vmem((nj, modes, LANES), WIRE),
            vmem((nj, modes, LANES), WIRE),
            vmem((ny, modes, LANES), F32),
            vmem((modes, LANES), F32),
            vmem((nj, modes, LANES), F32),
            vmem((nj, modes, LANES), F32),
            vmem((nj, modes, LANES), WIRE),
            vmem((nj, modes, LANES), WIRE),
            dma((7,)),
            dma((4,)),
            dma((nx,)),
            dma((nx,)),
            dma((nj,)),
            dma((nj,)),
            dma((ny,)),
            dma((ny,)),
            dma((nj,)),
            dma((nj,)),
        ],
        compiler_params=pltpu.CompilerParams(
            collective_id=0, has_side_effects=True, vmem_limit_bytes=40 * 1024 * 1024
        ),
    )(*[pltpu.with_memory_space_constraint(v, pltpu.HBM) for v in (
        stream,
        decay_rate.T,
        residue.T,
        norm_gain.reshape(blocks, LANES),
        skip_gain.reshape(blocks, LANES),
        gate_act,
        jnp.asarray(fwd),
        jnp.asarray(inv),
    )])


def solution(mesh):
    in_specs = (P("seq", "ch"), P("ch"), P("seq", "ch"), P("ch", None), P("ch", None), P("ch"))
    body = functools.partial(shards, mesh.shape["ch"], mesh.shape["seq"])
    return jax.shard_map(body, mesh=mesh, in_specs=in_specs, out_specs=P("seq", "ch"), check_vma=False)
```

```python
import functools
import math

import jax
import jax.numpy as jnp
import numpy as np
from jax import lax
from jax.experimental import pallas as pl
from jax.experimental.pallas import tpu as pltpu
from jax.sharding import PartitionSpec as P

MESH = pl.DeviceIdType.MESH
EPS = 1e-06
LANES = 128
WIRE = jnp.bfloat16
F32 = jnp.float32
BF16 = jnp.bfloat16


def half_tables(length):
    k = np.arange(length)[:, None] + 0.5
    t = np.arange(length)[None, :]
    angle = np.pi * k * t / length
    forward = np.concatenate([np.cos(angle), -np.sin(angle)], axis=0)
    inverse = np.concatenate([np.cos(angle.T), -np.sin(angle.T)], axis=1) / length

    def split(table):
        high = table.astype(BF16)
        low = (table - high.astype(np.float64)).astype(BF16)
        return np.concatenate([high, low], axis=1)

    return split(forward), split(inverse)


def one_minus_exp_neg(z):
    series = jnp.ones_like(z)
    for n in range(10, 1, -1):
        series = 1.0 - z * series * (1.0 / n)
    return jnp.where(z < 0.5, z * series, 1.0 - jnp.exp(-z))


def total_of(items):
    items = list(items)
    while len(items) > 1:
        items = [a + b for a, b in zip(items[::2], items[1::2])] + ([items[-1]] if len(items) % 2 else [])
    return items[0]


def rows_of(tile):
    return [jnp.broadcast_to(tile[m:m + 1, :], (8, LANES)) for m in range(tile.shape[0])]


def row_sums(tiles):
    row = lax.broadcasted_iota(jnp.int32, (8, LANES), 0)
    for bit in (4, 2, 1):
        clear = lax.rem(row // bit, 2) == 0
        count = len(tiles) // 2
        tiles = [jnp.where(clear, a + pltpu.roll(a, 8 - bit, 0), c + pltpu.roll(c, bit, 0))
                 for a, c in zip(tiles[:count], tiles[count:])]
    return tiles[0]


def kernel(nx, ny, nj, modes, width,
           x_hbm, rate_hbm, res_hbm, gain_hbm, skip_hbm, gate_hbm, fwd_hbm, inv_hbm, out_ref,
           x_v, gate_v, rate_v, res_v, gain_v, skip_v, fwd_v, inv_v,
           sqacc_v, sq_v, scol_v, pow_v, taps_v, conv_v, left_v, jump_v,
           st_out, st_in, tot_v, before_v, pre_v, fac_v, ca_out, ca_in,
           in_sem, x_sem, sq_send, sq_recv, st_send, st_recv, tot_send, tot_recv, ca_send, ca_recv):
    tokens, chans = x_v.shape
    blocks = chans // LANES
    mx = lax.axis_index("ch")
    seq = lax.axis_index("seq")
    my = seq // nj
    mj = lax.rem(seq, nj)

    def group_peer(k):
        return {"seq": my * nj + k}

    def spread(i):
        return nj // 2 + jnp.where(lax.rem(i, 2) == 1, (i + 1) // 2, -(i // 2))

    parts = x_sem.shape[0]
    rows_part = tokens // parts
    for p in range(parts):
        rows = pl.ds(p * rows_part, rows_part)
        pltpu.make_async_copy(x_hbm.at[rows], x_v.at[rows], x_sem.at[p]).start()
    staged = [(rate_hbm, rate_v), (res_hbm, res_v), (gain_hbm, gain_v), (skip_hbm, skip_v),
              (fwd_hbm, fwd_v), (inv_hbm, inv_v), (gate_hbm, gate_v)]
    staged = [pltpu.make_async_copy(a, b, in_sem.at[n]) for n, (a, b) in enumerate(staged)]
    for copy in staged:
        copy.start()

    half = nj // 2
    late = mj >= half
    barrier = pltpu.get_barrier_semaphore()
    for d in range(1, nx):
        pl.semaphore_signal(barrier, inc=1, device_id={"ch": lax.rem(mx + d, nx)}, device_id_type=MESH)
    for d in range(1, ny):
        pl.semaphore_signal(barrier, inc=1, device_id={"seq": lax.rem(seq + d * nj, ny * nj)}, device_id_type=MESH)

    def greet(first):
        for k in range(first, first + half):
            @pl.when(k != mj)
            def _():
                pl.semaphore_signal(barrier, inc=1, device_id=group_peer(k), device_id_type=MESH)

    @pl.when(late)
    def _():
        greet(half)

    tiles_part = rows_part // 16
    for p in range(parts):
        rows = pl.ds(p * rows_part, rows_part)
        pltpu.make_async_copy(x_hbm.at[rows], x_v.at[rows], x_sem.at[p]).wait()

        def square_rows(i, carry):
            part = pl.ds(pl.multiple_of(p * rows_part + i * 16, 16), 16)
            pieces = []
            for b in range(blocks):
                v = x_v[part, b * LANES:(b + 1) * LANES].astype(F32)
                pieces.append(v * v)
            sqacc_v[part, :] = total_of(pieces)
            return carry

        lax.fori_loop(0, tiles_part, square_rows, 0)
    turned = sqacc_v[...].T
    sq_v[mx] = total_of([turned[i * 8:(i + 1) * 8] for i in range(LANES // 8)])

    @pl.when(late)
    def _():
        pl.semaphore_wait(barrier, nx + ny + nj - 3)
        greet(0)

    @pl.when(jnp.logical_not(late))
    def _():
        pl.semaphore_wait(barrier, nx + ny - 2)
        greet(half)

    sq_copies = []
    for d in range(1, nx):
        copy = pltpu.make_async_remote_copy(
            src_ref=sq_v.at[mx], dst_ref=sq_v.at[mx], send_sem=sq_send.at[d], recv_sem=sq_recv.at[mx],
            device_id={"ch": lax.rem(mx + d, nx)}, device_id_type=MESH)
        copy.start()
        sq_copies.append(copy)

    for copy in staged[:6]:
        copy.wait()
    step8 = lax.broadcasted_iota(jnp.int32, (8, LANES), 0).astype(F32)

    def filter_block(b, carry):
        lanes = pl.ds(pl.multiple_of(b * LANES, LANES), LANES)
        rate = rate_v[:, lanes]
        weight = res_v[:, lanes] * jnp.sqrt(one_minus_exp_neg(2.0 * rate))
        jump = jnp.exp(-8.0 * rate)
        jump_v[:, lanes] = jump
        jump = rows_of(jump)
        terms = []
        for m in range(modes):
            power = jnp.exp(-rate[m:m + 1, :] * step8)
            pow_v[b * modes + m] = power
            left_v[b * modes + m] = jnp.exp(-rate[m:m + 1, :] * (7.0 - step8))
            terms.append(power * weight[m:m + 1, :])
        for t in range(tokens // 16):
            first = total_of(terms)
            terms = [a * c for a, c in zip(terms, jump)]
            second = total_of(terms)
            if t < tokens // 16 - 1:
                terms = [a * c for a, c in zip(terms, jump)]
            both = jnp.concatenate([first, second], axis=0)
            taps_v[t * 16:(t + 1) * 16, lanes] = both.astype(BF16)
        return carry

    lax.fori_loop(0, blocks, filter_block, 0)

    for d in range(1, nx):
        src = lax.rem(mx + d, nx)
        pltpu.make_async_remote_copy(
            src_ref=sq_v.at[src], dst_ref=sq_v.at[src], send_sem=sq_send.at[d], recv_sem=sq_recv.at[src],
            device_id={"ch": src}, device_id_type=MESH).wait_recv()
    squares = jnp.sum(total_of([sq_v[i] for i in range(nx)]), axis=0, keepdims=True)
    scale = lax.rsqrt(squares / (nx * chans) + EPS)
    scol_v[...] = jnp.broadcast_to(scale, (tokens, LANES)).T

    def state_copy(b):
        return pltpu.make_async_remote_copy(
            src_ref=st_out.at[b], dst_ref=st_in.at[mj], send_sem=st_send.at[b], recv_sem=st_recv.at[mj],
            device_id=group_peer(b), device_id_type=MESH)

    def state_of(b):
        lanes = pl.ds(pl.multiple_of(b * LANES, LANES), LANES)
        jump = rows_of(jump_v[:, lanes])
        sums = [None] * modes
        for t in range(tokens // 16):
            value = x_v[t * 16:(t + 1) * 16, lanes].astype(F32) * scol_v[t * 16:(t + 1) * 16, :]
            for part in (value[:8], value[8:]):
                sums = [part if s is None else s * c + part for s, c in zip(sums, jump)]
        sums = [s * left_v[b * modes + m] for m, s in enumerate(sums)]
        sums = jnp.concatenate([row_sums(sums[n:n + 8]) for n in range(0, modes, 8)], axis=0)
        st_out[b] = (sums * gain_v[pl.ds(b, 1), :]).astype(st_out.dtype)

    def state_blocks(i, carry):
        pair = [lax.rem(mj + spread(2 * i + n), nj) for n in range(2)]
        for b in pair:
            state_of(b)

        @pl.when(late)
        def _():
            state_copy(pair[0]).start()

            @pl.when(i < nj // 2 - 1)
            def _():
                state_copy(pair[1]).start()

        return carry

    lax.fori_loop(0, nj // 2, state_blocks, 0)
    st_in[mj] = st_out[mj]

    @pl.when(jnp.logical_not(late))
    def _():
        pl.semaphore_wait(barrier, nj // 2)

        def send_state(i, carry):
            k = nj - 1 - i

            @pl.when(k != mj)
            def _():
                state_copy(k).start()

            return carry

        lax.fori_loop(0, nj, send_state, 0)

    def local_conv(c, carry):
        lanes = pl.ds(pl.multiple_of(c * width, width), width)
        per = width // LANES
        scale = jnp.concatenate([scol_v[...]] * per, axis=1)
        gain = jnp.concatenate([gain_v[pl.ds(c * per + n, 1), :] for n in range(per)], axis=1)
        xn = (x_v[:, lanes].astype(F32) * scale * gain).astype(BF16)
        taps = taps_v[:, lanes]
        spec = jnp.dot(fwd_v[...], jnp.concatenate([xn, xn], axis=0), preferred_element_type=F32)
        filt = jnp.dot(fwd_v[...], jnp.concatenate([taps, taps], axis=0), preferred_element_type=F32)
        xr, xi = spec[:tokens], spec[tokens:]
        fr, fi = filt[:tokens], filt[tokens:]
        prod = jnp.concatenate([xr * fr - xi * fi, xr * fi + xi * fr], axis=0)
        prod = prod.astype(BF16)
        conv = jnp.dot(inv_v[...], jnp.concatenate([prod, prod], axis=0), preferred_element_type=F32)
        skip = jnp.concatenate([skip_v[pl.ds(c * per + n, 1), :] for n in range(per)], axis=1)
        conv_v[:, lanes] = conv + skip * xn.astype(F32)
        return carry

    chunks = chans // width
    cut1, cut2 = (3 * chunks) // 8, (4 * chunks) // 8
    lax.fori_loop(0, cut1, local_conv, 0)

    own = pl.ds(pl.multiple_of(mj * LANES, LANES), LANES)
    rate = rate_v[:, own]
    decay = jnp.exp(-float(tokens) * rate)

    def scan_group(k, state):
        @pl.when(k != mj)
        def _():
            pltpu.make_async_remote_copy(
                src_ref=st_out.at[k], dst_ref=st_in.at[k], send_sem=st_send.at[k], recv_sem=st_recv.at[k],
                device_id=group_peer(k), device_id_type=MESH).wait_recv()

        pre_v[k] = state
        return state * decay + st_in[k].astype(F32)

    tot_v[my] = lax.fori_loop(0, nj, scan_group, jnp.zeros((modes, LANES), F32))

    def total_copy(d):
        return pltpu.make_async_remote_copy(
            src_ref=tot_v.at[my], dst_ref=tot_v.at[my], send_sem=tot_send.at[d], recv_sem=tot_recv.at[my],
            device_id={"seq": lax.rem(seq + d * nj, ny * nj)}, device_id_type=MESH)

    for d in range(1, ny):
        @pl.when(my + d < ny)
        def _():
            total_copy(d).start()

    lax.fori_loop(cut1, cut2, local_conv, 0)

    scaled = res_v[:, own] * jnp.sqrt(one_minus_exp_neg(2.0 * rate)) * jnp.exp(-rate)
    shares = []
    for k in range(ny - 1):
        steps = jnp.maximum(my - 1 - k, 0) * (nj * tokens)
        shares.append(jnp.exp(-rate * steps.astype(F32)))

    def factors(k, carry):
        pre_v[k] = scaled * pre_v[k]
        fac_v[k] = scaled * jnp.exp(-rate * (k * tokens).astype(F32))
        return carry

    lax.fori_loop(0, nj, factors, 0)
    before_v[...] = jnp.zeros((modes, LANES), F32)
    for k in range(ny - 1):
        @pl.when(k < my)
        def _():
            pltpu.make_async_remote_copy(
                src_ref=tot_v.at[k], dst_ref=tot_v.at[k], send_sem=tot_send.at[1], recv_sem=tot_recv.at[k],
                device_id={"seq": k * nj + mj}, device_id_type=MESH).wait_recv()
            before_v[...] += shares[k] * tot_v[k]

    before = before_v[...]

    def carry_copy(k):
        return pltpu.make_async_remote_copy(
            src_ref=ca_out.at[k], dst_ref=ca_in.at[mj], send_sem=ca_send.at[k], recv_sem=ca_recv.at[mj],
            device_id=group_peer(k), device_id_type=MESH)

    def send_carry(k, carry):
        ca_out[k] = (pre_v[k] + fac_v[k] * before).astype(ca_out.dtype)

        @pl.when(k != mj)
        def _():
            carry_copy(k).start()

        return carry

    lax.fori_loop(0, nj, send_carry, 0)
    ca_in[mj] = ca_out[mj]

    lax.fori_loop(cut2, chunks, local_conv, 0)
    staged[6].wait()
    for copy in sq_copies:
        copy.wait_send()
    for d in range(1, ny):
        @pl.when(my + d < ny)
        def _():
            total_copy(d).wait_send()

    def drain_states(k, carry):
        @pl.when(k != mj)
        def _():
            state_copy(k).wait_send()

        return carry

    lax.fori_loop(0, nj, drain_states, 0)

    def await_block(b):

        @pl.when(b != mj)
        def _():
            pltpu.make_async_remote_copy(
                src_ref=ca_out.at[b], dst_ref=ca_in.at[b], send_sem=ca_send.at[b], recv_sem=ca_recv.at[b],
                device_id=group_peer(b), device_id_type=MESH).wait_recv()

    def finish(b):
        lanes = pl.ds(pl.multiple_of(b * LANES, LANES), LANES)
        jump = rows_of(jump_v[:, lanes])
        weight = ca_in[b].astype(F32)
        terms = [pow_v[b * modes + m] * weight[m:m + 1, :] for m in range(modes)]
        for t in range(tokens // 16):
            first = total_of(terms)
            terms = [a * c for a, c in zip(terms, jump)]
            second = total_of(terms)
            if t < tokens // 16 - 1:
                terms = [a * c for a, c in zip(terms, jump)]
            both = jnp.concatenate([first, second], axis=0) + conv_v[t * 16:(t + 1) * 16, lanes]
            gate = gate_v[t * 16:(t + 1) * 16, lanes].astype(F32)
            out_ref[t * 16:(t + 1) * 16, lanes] = (both * gate).astype(BF16)

    def finish_blocks(i, carry):
        pair = [lax.rem(mj + 2 * nj - spread(nj - 1 - 2 * i - n), nj) for n in range(2)]
        for b in pair:
            await_block(b)
        for b in pair:
            finish(b)
        return carry

    def drain_carries(k, carry):
        @pl.when(k != mj)
        def _():
            carry_copy(k).wait_send()

        return carry

    lax.fori_loop(0, blocks // 8, finish_blocks, 0)
    lax.fori_loop(0, nj, drain_carries, 0)
    lax.fori_loop(blocks // 8, blocks // 2, finish_blocks, 0)


def shards(nx, nseq, stream, norm_gain, gate_act, decay_rate, residue, skip_gain):
    tokens, chans = stream.shape
    modes = decay_rate.shape[1]
    blocks = chans // LANES
    nj = blocks
    ny = nseq // nj
    width = 256
    fwd, inv = half_tables(tokens)
    any_spec = pl.BlockSpec(memory_space=pl.ANY)
    vmem = pltpu.VMEM
    dma = pltpu.SemaphoreType.DMA
    return pl.pallas_call(
        functools.partial(kernel, nx, ny, nj, modes, width),
        out_shape=jax.ShapeDtypeStruct((tokens, chans), BF16),
        in_specs=[any_spec] * 8,
        out_specs=pl.BlockSpec(memory_space=pltpu.VMEM),
        scratch_shapes=[
            vmem((tokens, chans), BF16),
            vmem((tokens, chans), BF16),
            vmem((modes, chans), F32),
            vmem((modes, chans), F32),
            vmem((blocks, LANES), F32),
            vmem((blocks, LANES), F32),
            vmem(fwd.shape, BF16),
            vmem(inv.shape, BF16),
            vmem((tokens, LANES), F32),
            vmem((nx, 8, LANES), F32),
            vmem((tokens, LANES), F32),
            vmem((blocks * modes, 8, LANES), F32),
            vmem((tokens, chans), BF16),
            vmem((tokens, chans), F32),
            vmem((blocks * modes, 8, LANES), F32),
            vmem((modes, chans), F32),
            vmem((nj, modes, LANES), WIRE),
            vmem((nj, modes, LANES), WIRE),
            vmem((ny, modes, LANES), F32),
            vmem((modes, LANES), F32),
            vmem((nj, modes, LANES), F32),
            vmem((nj, modes, LANES), F32),
            vmem((nj, modes, LANES), WIRE),
            vmem((nj, modes, LANES), WIRE),
            dma((7,)),
            dma((4,)),
            dma((nx,)),
            dma((nx,)),
            dma((nj,)),
            dma((nj,)),
            dma((ny,)),
            dma((ny,)),
            dma((nj,)),
            dma((nj,)),
        ],
        compiler_params=pltpu.CompilerParams(
            collective_id=0, has_side_effects=True, vmem_limit_bytes=40 * 1024 * 1024
        ),
    )(*[pltpu.with_memory_space_constraint(v, pltpu.HBM) for v in (
        stream,
        decay_rate.T,
        residue.T,
        norm_gain.reshape(blocks, LANES),
        skip_gain.reshape(blocks, LANES),
        gate_act,
        jnp.asarray(fwd),
        jnp.asarray(inv),
    )])


def solution(mesh):
    in_specs = (P("seq", "ch"), P("ch"), P("seq", "ch"), P("ch", None), P("ch", None), P("ch"))
    body = functools.partial(shards, mesh.shape["ch"], mesh.shape["seq"])
    return jax.shard_map(body, mesh=mesh, in_specs=in_specs, out_specs=P("seq", "ch"), check_vma=False)
```

```python
import functools
import math

import jax
import jax.numpy as jnp
import numpy as np
from jax import lax
from jax.experimental import pallas as pl
from jax.experimental.pallas import tpu as pltpu
from jax.sharding import PartitionSpec as P

MESH = pl.DeviceIdType.MESH
EPS = 1e-06
LANES = 128
WIRE = jnp.bfloat16
F32 = jnp.float32
BF16 = jnp.bfloat16


def half_tables(length):
    k = np.arange(length)[:, None] + 0.5
    t = np.arange(length)[None, :]
    angle = np.pi * k * t / length
    forward = np.concatenate([np.cos(angle), -np.sin(angle)], axis=0)
    inverse = np.concatenate([np.cos(angle.T), -np.sin(angle.T)], axis=1) / length

    def split(table):
        high = table.astype(BF16)
        low = (table - high.astype(np.float64)).astype(BF16)
        return np.concatenate([high, low], axis=1)

    return split(forward), split(inverse)


def one_minus_exp_neg(z):
    series = jnp.ones_like(z)
    for n in range(10, 1, -1):
        series = 1.0 - z * series * (1.0 / n)
    return jnp.where(z < 0.5, z * series, 1.0 - jnp.exp(-z))


def total_of(items):
    items = list(items)
    while len(items) > 1:
        items = [a + b for a, b in zip(items[::2], items[1::2])] + ([items[-1]] if len(items) % 2 else [])
    return items[0]


def rows_of(tile):
    return [jnp.broadcast_to(tile[m:m + 1, :], (8, LANES)) for m in range(tile.shape[0])]


def row_sums(tiles):
    row = lax.broadcasted_iota(jnp.int32, (8, LANES), 0)
    for bit in (4, 2, 1):
        clear = lax.rem(row // bit, 2) == 0
        count = len(tiles) // 2
        tiles = [jnp.where(clear, a + pltpu.roll(a, 8 - bit, 0), c + pltpu.roll(c, bit, 0))
                 for a, c in zip(tiles[:count], tiles[count:])]
    return tiles[0]


def kernel(nx, ny, nj, modes, width,
           x_hbm, rate_hbm, res_hbm, gain_hbm, skip_hbm, gate_hbm, fwd_hbm, inv_hbm, out_ref,
           x_v, gate_v, rate_v, res_v, gain_v, skip_v, fwd_v, inv_v,
           sqacc_v, sq_v, scol_v, pow_v, taps_v, conv_v, left_v, jump_v,
           st_out, st_in, tot_v, before_v, pre_v, fac_v, ca_out, ca_in,
           in_sem, x_sem, sq_send, sq_recv, st_send, st_recv, tot_send, tot_recv, ca_send, ca_recv):
    tokens, chans = x_v.shape
    blocks = chans // LANES
    mx = lax.axis_index("ch")
    seq = lax.axis_index("seq")
    my = seq // nj
    mj = lax.rem(seq, nj)

    def group_peer(k):
        return {"seq": my * nj + k}

    def spread(i):
        return nj // 2 + jnp.where(lax.rem(i, 2) == 1, (i + 1) // 2, -(i // 2))

    parts = x_sem.shape[0]
    rows_part = tokens // parts
    for p in range(parts):
        rows = pl.ds(p * rows_part, rows_part)
        pltpu.make_async_copy(x_hbm.at[rows], x_v.at[rows], x_sem.at[p]).start()
    staged = [(rate_hbm, rate_v), (res_hbm, res_v), (gain_hbm, gain_v), (skip_hbm, skip_v),
              (fwd_hbm, fwd_v), (inv_hbm, inv_v), (gate_hbm, gate_v)]
    staged = [pltpu.make_async_copy(a, b, in_sem.at[n]) for n, (a, b) in enumerate(staged)]
    for copy in staged:
        copy.start()

    half = nj // 2
    late = mj >= half
    barrier = pltpu.get_barrier_semaphore()
    for d in range(1, nx):
        pl.semaphore_signal(barrier, inc=1, device_id={"ch": lax.rem(mx + d, nx)}, device_id_type=MESH)
    for d in range(1, ny):
        pl.semaphore_signal(barrier, inc=1, device_id={"seq": lax.rem(seq + d * nj, ny * nj)}, device_id_type=MESH)

    def greet(first):
        for k in range(first, first + half):
            @pl.when(k != mj)
            def _():
                pl.semaphore_signal(barrier, inc=1, device_id=group_peer(k), device_id_type=MESH)

    @pl.when(late)
    def _():
        greet(half)

    @pl.when(jnp.logical_not(late))
    def _():
        pl.semaphore_wait(barrier, nx + ny - 2)
        greet(half)

    tiles_part = rows_part // 16
    for p in range(parts):
        rows = pl.ds(p * rows_part, rows_part)
        pltpu.make_async_copy(x_hbm.at[rows], x_v.at[rows], x_sem.at[p]).wait()

        def square_rows(i, carry):
            part = pl.ds(pl.multiple_of(p * rows_part + i * 16, 16), 16)
            pieces = []
            for b in range(blocks):
                v = x_v[part, b * LANES:(b + 1) * LANES].astype(F32)
                pieces.append(v * v)
            sqacc_v[part, :] = total_of(pieces)
            return carry

        lax.fori_loop(0, tiles_part, square_rows, 0)
    turned = sqacc_v[...].T
    sq_v[mx] = total_of([turned[i * 8:(i + 1) * 8] for i in range(LANES // 8)])

    @pl.when(late)
    def _():
        pl.semaphore_wait(barrier, nx + ny + nj - 3)
        greet(0)

    sq_copies = []
    for d in range(1, nx):
        copy = pltpu.make_async_remote_copy(
            src_ref=sq_v.at[mx], dst_ref=sq_v.at[mx], send_sem=sq_send.at[d], recv_sem=sq_recv.at[mx],
            device_id={"ch": lax.rem(mx + d, nx)}, device_id_type=MESH)
        copy.start()
        sq_copies.append(copy)

    for copy in staged[:6]:
        copy.wait()
    step8 = lax.broadcasted_iota(jnp.int32, (8, LANES), 0).astype(F32)

    def filter_block(b, carry):
        lanes = pl.ds(pl.multiple_of(b * LANES, LANES), LANES)
        rate = rate_v[:, lanes]
        weight = res_v[:, lanes] * jnp.sqrt(one_minus_exp_neg(2.0 * rate))
        jump = jnp.exp(-8.0 * rate)
        jump_v[:, lanes] = jump
        jump = rows_of(jump)
        terms = []
        for m in range(modes):
            power = jnp.exp(-rate[m:m + 1, :] * step8)
            pow_v[b * modes + m] = power
            left_v[b * modes + m] = jnp.exp(-rate[m:m + 1, :] * (7.0 - step8))
            terms.append(power * weight[m:m + 1, :])
        for t in range(tokens // 16):
            first = total_of(terms)
            terms = [a * c for a, c in zip(terms, jump)]
            second = total_of(terms)
            if t < tokens // 16 - 1:
                terms = [a * c for a, c in zip(terms, jump)]
            both = jnp.concatenate([first, second], axis=0)
            taps_v[t * 16:(t + 1) * 16, lanes] = both.astype(BF16)
        return carry

    lax.fori_loop(0, blocks, filter_block, 0)

    for d in range(1, nx):
        src = lax.rem(mx + d, nx)
        pltpu.make_async_remote_copy(
            src_ref=sq_v.at[src], dst_ref=sq_v.at[src], send_sem=sq_send.at[d], recv_sem=sq_recv.at[src],
            device_id={"ch": src}, device_id_type=MESH).wait_recv()
    squares = jnp.sum(total_of([sq_v[i] for i in range(nx)]), axis=0, keepdims=True)
    scale = lax.rsqrt(squares / (nx * chans) + EPS)
    scol_v[...] = jnp.broadcast_to(scale, (tokens, LANES)).T

    def state_copy(b):
        return pltpu.make_async_remote_copy(
            src_ref=st_out.at[b], dst_ref=st_in.at[mj], send_sem=st_send.at[b], recv_sem=st_recv.at[mj],
            device_id=group_peer(b), device_id_type=MESH)

    def state_of(b):
        lanes = pl.ds(pl.multiple_of(b * LANES, LANES), LANES)
        jump = rows_of(jump_v[:, lanes])
        sums = [None] * modes
        for t in range(tokens // 16):
            value = x_v[t * 16:(t + 1) * 16, lanes].astype(F32) * scol_v[t * 16:(t + 1) * 16, :]
            for part in (value[:8], value[8:]):
                sums = [part if s is None else s * c + part for s, c in zip(sums, jump)]
        sums = [s * left_v[b * modes + m] for m, s in enumerate(sums)]
        sums = jnp.concatenate([row_sums(sums[n:n + 8]) for n in range(0, modes, 8)], axis=0)
        st_out[b] = (sums * gain_v[pl.ds(b, 1), :]).astype(st_out.dtype)

    def state_blocks(i, carry):
        pair = [lax.rem(mj + spread(2 * i + n), nj) for n in range(2)]
        for b in pair:
            state_of(b)

        @pl.when(late)
        def _():
            state_copy(pair[0]).start()

            @pl.when(i < nj // 2 - 1)
            def _():
                state_copy(pair[1]).start()

        return carry

    lax.fori_loop(0, nj // 2, state_blocks, 0)
    st_in[mj] = st_out[mj]

    @pl.when(jnp.logical_not(late))
    def _():
        pl.semaphore_wait(barrier, nj // 2)

        def send_state(i, carry):
            k = nj - 1 - i

            @pl.when(k != mj)
            def _():
                state_copy(k).start()

            return carry

        lax.fori_loop(0, nj, send_state, 0)

    def local_conv(c, carry):
        lanes = pl.ds(pl.multiple_of(c * width, width), width)
        per = width // LANES
        scale = jnp.concatenate([scol_v[...]] * per, axis=1)
        gain = jnp.concatenate([gain_v[pl.ds(c * per + n, 1), :] for n in range(per)], axis=1)
        xn = (x_v[:, lanes].astype(F32) * scale * gain).astype(BF16)
        taps = taps_v[:, lanes]
        spec = jnp.dot(fwd_v[...], jnp.concatenate([xn, xn], axis=0), preferred_element_type=F32)
        filt = jnp.dot(fwd_v[...], jnp.concatenate([taps, taps], axis=0), preferred_element_type=F32)
        xr, xi = spec[:tokens], spec[tokens:]
        fr, fi = filt[:tokens], filt[tokens:]
        prod = jnp.concatenate([xr * fr - xi * fi, xr * fi + xi * fr], axis=0)
        prod = prod.astype(BF16)
        conv = jnp.dot(inv_v[...], jnp.concatenate([prod, prod], axis=0), preferred_element_type=F32)
        skip = jnp.concatenate([skip_v[pl.ds(c * per + n, 1), :] for n in range(per)], axis=1)
        conv_v[:, lanes] = conv + skip * xn.astype(F32)
        return carry

    chunks = chans // width
    cut1, cut2 = (3 * chunks) // 8, (3 * chunks) // 8
    lax.fori_loop(0, cut1, local_conv, 0)

    own = pl.ds(pl.multiple_of(mj * LANES, LANES), LANES)
    rate = rate_v[:, own]
    decay = jnp.exp(-float(tokens) * rate)

    def scan_group(k, state):
        @pl.when(k != mj)
        def _():
            pltpu.make_async_remote_copy(
                src_ref=st_out.at[k], dst_ref=st_in.at[k], send_sem=st_send.at[k], recv_sem=st_recv.at[k],
                device_id=group_peer(k), device_id_type=MESH).wait_recv()

        pre_v[k] = state
        return state * decay + st_in[k].astype(F32)

    tot_v[my] = lax.fori_loop(0, nj, scan_group, jnp.zeros((modes, LANES), F32))

    def total_copy(d):
        return pltpu.make_async_remote_copy(
            src_ref=tot_v.at[my], dst_ref=tot_v.at[my], send_sem=tot_send.at[d], recv_sem=tot_recv.at[my],
            device_id={"seq": lax.rem(seq + d * nj, ny * nj)}, device_id_type=MESH)

    for d in range(1, ny):
        @pl.when(my + d < ny)
        def _():
            total_copy(d).start()

    lax.fori_loop(cut1, cut2, local_conv, 0)

    scaled = res_v[:, own] * jnp.sqrt(one_minus_exp_neg(2.0 * rate)) * jnp.exp(-rate)
    shares = []
    for k in range(ny - 1):
        steps = jnp.maximum(my - 1 - k, 0) * (nj * tokens)
        shares.append(jnp.exp(-rate * steps.astype(F32)))

    def factors(k, carry):
        pre_v[k] = scaled * pre_v[k]
        fac_v[k] = scaled * jnp.exp(-rate * (k * tokens).astype(F32))
        return carry

    lax.fori_loop(0, nj, factors, 0)
    before_v[...] = jnp.zeros((modes, LANES), F32)
    for k in range(ny - 1):
        @pl.when(k < my)
        def _():
            pltpu.make_async_remote_copy(
                src_ref=tot_v.at[k], dst_ref=tot_v.at[k], send_sem=tot_send.at[1], recv_sem=tot_recv.at[k],
                device_id={"seq": k * nj + mj}, device_id_type=MESH).wait_recv()
            before_v[...] += shares[k] * tot_v[k]

    before = before_v[...]

    def carry_copy(k):
        return pltpu.make_async_remote_copy(
            src_ref=ca_out.at[k], dst_ref=ca_in.at[mj], send_sem=ca_send.at[k], recv_sem=ca_recv.at[mj],
            device_id=group_peer(k), device_id_type=MESH)

    def send_carry(k, carry):
        ca_out[k] = (pre_v[k] + fac_v[k] * before).astype(ca_out.dtype)

        @pl.when(k != mj)
        def _():
            carry_copy(k).start()

        return carry

    lax.fori_loop(0, nj, send_carry, 0)
    ca_in[mj] = ca_out[mj]

    lax.fori_loop(cut2, chunks, local_conv, 0)
    staged[6].wait()
    for copy in sq_copies:
        copy.wait_send()
    for d in range(1, ny):
        @pl.when(my + d < ny)
        def _():
            total_copy(d).wait_send()

    def drain_states(k, carry):
        @pl.when(k != mj)
        def _():
            state_copy(k).wait_send()

        return carry

    lax.fori_loop(0, nj, drain_states, 0)

    def await_block(b):

        @pl.when(b != mj)
        def _():
            pltpu.make_async_remote_copy(
                src_ref=ca_out.at[b], dst_ref=ca_in.at[b], send_sem=ca_send.at[b], recv_sem=ca_recv.at[b],
                device_id=group_peer(b), device_id_type=MESH).wait_recv()

    def finish(b):
        lanes = pl.ds(pl.multiple_of(b * LANES, LANES), LANES)
        jump = rows_of(jump_v[:, lanes])
        weight = ca_in[b].astype(F32)
        terms = [pow_v[b * modes + m] * weight[m:m + 1, :] for m in range(modes)]
        for t in range(tokens // 16):
            first = total_of(terms)
            terms = [a * c for a, c in zip(terms, jump)]
            second = total_of(terms)
            if t < tokens // 16 - 1:
                terms = [a * c for a, c in zip(terms, jump)]
            both = jnp.concatenate([first, second], axis=0) + conv_v[t * 16:(t + 1) * 16, lanes]
            gate = gate_v[t * 16:(t + 1) * 16, lanes].astype(F32)
            out_ref[t * 16:(t + 1) * 16, lanes] = (both * gate).astype(BF16)

    def finish_blocks(i, carry):
        pair = [lax.rem(mj + 2 * nj - spread(nj - 1 - 2 * i - n), nj) for n in range(2)]
        for b in pair:
            await_block(b)
        for b in pair:
            finish(b)
        return carry

    def drain_carries(k, carry):
        @pl.when(k != mj)
        def _():
            carry_copy(k).wait_send()

        return carry

    lax.fori_loop(0, blocks // 8, finish_blocks, 0)
    lax.fori_loop(0, nj, drain_carries, 0)
    lax.fori_loop(blocks // 8, blocks // 2, finish_blocks, 0)


def shards(nx, nseq, stream, norm_gain, gate_act, decay_rate, residue, skip_gain):
    tokens, chans = stream.shape
    modes = decay_rate.shape[1]
    blocks = chans // LANES
    nj = blocks
    ny = nseq // nj
    width = 256
    fwd, inv = half_tables(tokens)
    any_spec = pl.BlockSpec(memory_space=pl.ANY)
    vmem = pltpu.VMEM
    dma = pltpu.SemaphoreType.DMA
    return pl.pallas_call(
        functools.partial(kernel, nx, ny, nj, modes, width),
        out_shape=jax.ShapeDtypeStruct((tokens, chans), BF16),
        in_specs=[any_spec] * 8,
        out_specs=pl.BlockSpec(memory_space=pltpu.VMEM),
        scratch_shapes=[
            vmem((tokens, chans), BF16),
            vmem((tokens, chans), BF16),
            vmem((modes, chans), F32),
            vmem((modes, chans), F32),
            vmem((blocks, LANES), F32),
            vmem((blocks, LANES), F32),
            vmem(fwd.shape, BF16),
            vmem(inv.shape, BF16),
            vmem((tokens, LANES), F32),
            vmem((nx, 8, LANES), F32),
            vmem((tokens, LANES), F32),
            vmem((blocks * modes, 8, LANES), F32),
            vmem((tokens, chans), BF16),
            vmem((tokens, chans), F32),
            vmem((blocks * modes, 8, LANES), F32),
            vmem((modes, chans), F32),
            vmem((nj, modes, LANES), WIRE),
            vmem((nj, modes, LANES), WIRE),
            vmem((ny, modes, LANES), F32),
            vmem((modes, LANES), F32),
            vmem((nj, modes, LANES), F32),
            vmem((nj, modes, LANES), F32),
            vmem((nj, modes, LANES), WIRE),
            vmem((nj, modes, LANES), WIRE),
            dma((7,)),
            dma((4,)),
            dma((nx,)),
            dma((nx,)),
            dma((nj,)),
            dma((nj,)),
            dma((ny,)),
            dma((ny,)),
            dma((nj,)),
            dma((nj,)),
        ],
        compiler_params=pltpu.CompilerParams(
            collective_id=0, has_side_effects=True, vmem_limit_bytes=40 * 1024 * 1024
        ),
    )(*[pltpu.with_memory_space_constraint(v, pltpu.HBM) for v in (
        stream,
        decay_rate.T,
        residue.T,
        norm_gain.reshape(blocks, LANES),
        skip_gain.reshape(blocks, LANES),
        gate_act,
        jnp.asarray(fwd),
        jnp.asarray(inv),
    )])


def solution(mesh):
    in_specs = (P("seq", "ch"), P("ch"), P("seq", "ch"), P("ch", None), P("ch", None), P("ch"))
    body = functools.partial(shards, mesh.shape["ch"], mesh.shape["seq"])
    return jax.shard_map(body, mesh=mesh, in_specs=in_specs, out_specs=P("seq", "ch"), check_vma=False)
```

```python
import functools
import math

import jax
import jax.numpy as jnp
import numpy as np
from jax import lax
from jax.experimental import pallas as pl
from jax.experimental.pallas import tpu as pltpu
from jax.sharding import PartitionSpec as P

MESH = pl.DeviceIdType.MESH
EPS = 1e-06
LANES = 128
WIRE = jnp.bfloat16
F32 = jnp.float32
BF16 = jnp.bfloat16


def half_tables(length):
    k = np.arange(length)[:, None] + 0.5
    t = np.arange(length)[None, :]
    angle = np.pi * k * t / length
    forward = np.concatenate([np.cos(angle), -np.sin(angle)], axis=0)
    inverse = np.concatenate([np.cos(angle.T), -np.sin(angle.T)], axis=1) / length

    def split(table):
        high = table.astype(BF16)
        low = (table - high.astype(np.float64)).astype(BF16)
        return np.concatenate([high, low], axis=1)

    return split(forward), split(inverse)


def one_minus_exp_neg(z):
    series = jnp.ones_like(z)
    for n in range(10, 1, -1):
        series = 1.0 - z * series * (1.0 / n)
    return jnp.where(z < 0.5, z * series, 1.0 - jnp.exp(-z))


def total_of(items):
    items = list(items)
    while len(items) > 1:
        items = [a + b for a, b in zip(items[::2], items[1::2])] + ([items[-1]] if len(items) % 2 else [])
    return items[0]


def rows_of(tile):
    return [jnp.broadcast_to(tile[m:m + 1, :], (8, LANES)) for m in range(tile.shape[0])]


def row_sums(tiles):
    row = lax.broadcasted_iota(jnp.int32, (8, LANES), 0)
    for bit in (4, 2, 1):
        clear = lax.rem(row // bit, 2) == 0
        count = len(tiles) // 2
        tiles = [jnp.where(clear, a + pltpu.roll(a, 8 - bit, 0), c + pltpu.roll(c, bit, 0))
                 for a, c in zip(tiles[:count], tiles[count:])]
    return tiles[0]


def kernel(nx, ny, nj, modes, width,
           x_hbm, rate_hbm, res_hbm, gain_hbm, skip_hbm, gate_hbm, fwd_hbm, inv_hbm, out_ref,
           x_v, gate_v, rate_v, res_v, gain_v, skip_v, fwd_v, inv_v,
           sqacc_v, sq_v, scol_v, pow_v, taps_v, conv_v, left_v, jump_v,
           st_out, st_in, tot_v, before_v, pre_v, fac_v, ca_out, ca_in,
           in_sem, x_sem, sq_send, sq_recv, st_send, st_recv, tot_send, tot_recv, ca_send, ca_recv):
    tokens, chans = x_v.shape
    blocks = chans // LANES
    mx = lax.axis_index("ch")
    seq = lax.axis_index("seq")
    my = seq // nj
    mj = lax.rem(seq, nj)

    def group_peer(k):
        return {"seq": my * nj + k}

    def spread(i):
        return nj // 2 + jnp.where(lax.rem(i, 2) == 1, (i + 1) // 2, -(i // 2))

    parts = x_sem.shape[0]
    rows_part = tokens // parts
    for p in range(parts):
        rows = pl.ds(p * rows_part, rows_part)
        pltpu.make_async_copy(x_hbm.at[rows], x_v.at[rows], x_sem.at[p]).start()
    staged = [(rate_hbm, rate_v), (res_hbm, res_v), (gain_hbm, gain_v), (skip_hbm, skip_v),
              (fwd_hbm, fwd_v), (inv_hbm, inv_v), (gate_hbm, gate_v)]
    staged = [pltpu.make_async_copy(a, b, in_sem.at[n]) for n, (a, b) in enumerate(staged)]
    for copy in staged:
        copy.start()

    half = nj // 2
    late = mj >= half
    barrier = pltpu.get_barrier_semaphore()
    for d in range(1, nx):
        pl.semaphore_signal(barrier, inc=1, device_id={"ch": lax.rem(mx + d, nx)}, device_id_type=MESH)
    for d in range(1, ny):
        pl.semaphore_signal(barrier, inc=1, device_id={"seq": lax.rem(seq + d * nj, ny * nj)}, device_id_type=MESH)

    def greet(first):
        for k in range(first, first + half):
            @pl.when(k != mj)
            def _():
                pl.semaphore_signal(barrier, inc=1, device_id=group_peer(k), device_id_type=MESH)

    @pl.when(late)
    def _():
        greet(half)

    @pl.when(jnp.logical_not(late))
    def _():
        pl.semaphore_wait(barrier, nx + ny - 2)
        greet(half)

    tiles_part = rows_part // 16
    for p in range(parts):
        rows = pl.ds(p * rows_part, rows_part)
        pltpu.make_async_copy(x_hbm.at[rows], x_v.at[rows], x_sem.at[p]).wait()

        def square_rows(i, carry):
            part = pl.ds(pl.multiple_of(p * rows_part + i * 16, 16), 16)
            pieces = []
            for b in range(blocks):
                v = x_v[part, b * LANES:(b + 1) * LANES].astype(F32)
                pieces.append(v * v)
            sqacc_v[part, :] = total_of(pieces)
            return carry

        lax.fori_loop(0, tiles_part, square_rows, 0)
    turned = sqacc_v[...].T
    sq_v[mx] = total_of([turned[i * 8:(i + 1) * 8] for i in range(LANES // 8)])

    @pl.when(late)
    def _():
        pl.semaphore_wait(barrier, nx + ny + nj - 3)
        greet(0)

    sq_copies = []
    for d in range(1, nx):
        copy = pltpu.make_async_remote_copy(
            src_ref=sq_v.at[mx], dst_ref=sq_v.at[mx], send_sem=sq_send.at[d], recv_sem=sq_recv.at[mx],
            device_id={"ch": lax.rem(mx + d, nx)}, device_id_type=MESH)
        copy.start()
        sq_copies.append(copy)

    for copy in staged[:6]:
        copy.wait()
    step8 = lax.broadcasted_iota(jnp.int32, (8, LANES), 0).astype(F32)

    def filter_block(b, carry):
        lanes = pl.ds(pl.multiple_of(b * LANES, LANES), LANES)
        rate = rate_v[:, lanes]
        weight = res_v[:, lanes] * jnp.sqrt(one_minus_exp_neg(2.0 * rate))
        jump = jnp.exp(-8.0 * rate)
        jump_v[:, lanes] = jump
        jump = rows_of(jump)
        terms = []
        for m in range(modes):
            power = jnp.exp(-rate[m:m + 1, :] * step8)
            pow_v[b * modes + m] = power
            left_v[b * modes + m] = jnp.exp(-rate[m:m + 1, :] * (7.0 - step8))
            terms.append(power * weight[m:m + 1, :])
        for t in range(tokens // 16):
            first = total_of(terms)
            terms = [a * c for a, c in zip(terms, jump)]
            second = total_of(terms)
            if t < tokens // 16 - 1:
                terms = [a * c for a, c in zip(terms, jump)]
            both = jnp.concatenate([first, second], axis=0)
            taps_v[t * 16:(t + 1) * 16, lanes] = both.astype(BF16)
        return carry

    lax.fori_loop(0, blocks, filter_block, 0)

    for d in range(1, nx):
        src = lax.rem(mx + d, nx)
        pltpu.make_async_remote_copy(
            src_ref=sq_v.at[src], dst_ref=sq_v.at[src], send_sem=sq_send.at[d], recv_sem=sq_recv.at[src],
            device_id={"ch": src}, device_id_type=MESH).wait_recv()
    squares = jnp.sum(total_of([sq_v[i] for i in range(nx)]), axis=0, keepdims=True)
    scale = lax.rsqrt(squares / (nx * chans) + EPS)
    scol_v[...] = jnp.broadcast_to(scale, (tokens, LANES)).T

    def state_copy(b):
        return pltpu.make_async_remote_copy(
            src_ref=st_out.at[b], dst_ref=st_in.at[mj], send_sem=st_send.at[b], recv_sem=st_recv.at[mj],
            device_id=group_peer(b), device_id_type=MESH)

    def state_of(b):
        lanes = pl.ds(pl.multiple_of(b * LANES, LANES), LANES)
        jump = rows_of(jump_v[:, lanes])
        sums = [None] * modes
        for t in range(tokens // 16):
            value = x_v[t * 16:(t + 1) * 16, lanes].astype(F32) * scol_v[t * 16:(t + 1) * 16, :]
            for part in (value[:8], value[8:]):
                sums = [part if s is None else s * c + part for s, c in zip(sums, jump)]
        sums = [s * left_v[b * modes + m] for m, s in enumerate(sums)]
        sums = jnp.concatenate([row_sums(sums[n:n + 8]) for n in range(0, modes, 8)], axis=0)
        st_out[b] = (sums * gain_v[pl.ds(b, 1), :]).astype(st_out.dtype)

    def state_blocks(i, carry):
        pair = [lax.rem(mj + spread(2 * i + n), nj) for n in range(2)]
        for b in pair:
            state_of(b)

        @pl.when(late)
        def _():
            state_copy(pair[0]).start()

            @pl.when(i < nj // 2 - 1)
            def _():
                state_copy(pair[1]).start()

        return carry

    lax.fori_loop(0, nj // 2, state_blocks, 0)
    st_in[mj] = st_out[mj]

    @pl.when(jnp.logical_not(late))
    def _():
        pl.semaphore_wait(barrier, nj // 2)

        def send_state(i, carry):
            k = nj - 1 - i

            @pl.when(k != mj)
            def _():
                state_copy(k).start()

            return carry

        lax.fori_loop(0, nj, send_state, 0)

    def local_conv(c, carry):
        lanes = pl.ds(pl.multiple_of(c * width, width), width)
        per = width // LANES
        scale = jnp.concatenate([scol_v[...]] * per, axis=1)
        gain = jnp.concatenate([gain_v[pl.ds(c * per + n, 1), :] for n in range(per)], axis=1)
        xn = (x_v[:, lanes].astype(F32) * scale * gain).astype(BF16)
        taps = taps_v[:, lanes]
        spec = jnp.dot(fwd_v[...], jnp.concatenate([xn, xn], axis=0), preferred_element_type=F32)
        filt = jnp.dot(fwd_v[...], jnp.concatenate([taps, taps], axis=0), preferred_element_type=F32)
        xr, xi = spec[:tokens], spec[tokens:]
        fr, fi = filt[:tokens], filt[tokens:]
        prod = jnp.concatenate([xr * fr - xi * fi, xr * fi + xi * fr], axis=0)
        prod = prod.astype(BF16)
        conv = jnp.dot(inv_v[...], jnp.concatenate([prod, prod], axis=0), preferred_element_type=F32)
        skip = jnp.concatenate([skip_v[pl.ds(c * per + n, 1), :] for n in range(per)], axis=1)
        conv_v[:, lanes] = conv + skip * xn.astype(F32)
        return carry

    chunks = chans // width
    cut1, cut2 = (3 * chunks) // 8, (3 * chunks) // 8
    lax.fori_loop(0, cut1, local_conv, 0)

    own = pl.ds(pl.multiple_of(mj * LANES, LANES), LANES)
    rate = rate_v[:, own]
    decay = jnp.exp(-float(tokens) * rate)

    def scan_group(k, state):
        @pl.when(k != mj)
        def _():
            pltpu.make_async_remote_copy(
                src_ref=st_out.at[k], dst_ref=st_in.at[k], send_sem=st_send.at[k], recv_sem=st_recv.at[k],
                device_id=group_peer(k), device_id_type=MESH).wait_recv()

        pre_v[k] = state
        return state * decay + st_in[k].astype(F32)

    tot_v[my] = lax.fori_loop(0, nj, scan_group, jnp.zeros((modes, LANES), F32))

    def total_copy(d):
        return pltpu.make_async_remote_copy(
            src_ref=tot_v.at[my], dst_ref=tot_v.at[my], send_sem=tot_send.at[d], recv_sem=tot_recv.at[my],
            device_id={"seq": lax.rem(seq + d * nj, ny * nj)}, device_id_type=MESH)

    for d in range(1, ny):
        @pl.when(my + d < ny)
        def _():
            total_copy(d).start()

    lax.fori_loop(cut1, cut2, local_conv, 0)

    scaled = res_v[:, own] * jnp.sqrt(one_minus_exp_neg(2.0 * rate)) * jnp.exp(-rate)
    shares = []
    for k in range(ny - 1):
        steps = jnp.maximum(my - 1 - k, 0) * (nj * tokens)
        shares.append(jnp.exp(-rate * steps.astype(F32)))

    def factors(k, carry):
        pre_v[k] = scaled * pre_v[k]
        fac_v[k] = scaled * jnp.exp(-rate * (k * tokens).astype(F32))
        return carry

    lax.fori_loop(0, nj, factors, 0)
    before_v[...] = jnp.zeros((modes, LANES), F32)
    for k in range(ny - 1):
        @pl.when(k < my)
        def _():
            pltpu.make_async_remote_copy(
                src_ref=tot_v.at[k], dst_ref=tot_v.at[k], send_sem=tot_send.at[1], recv_sem=tot_recv.at[k],
                device_id={"seq": k * nj + mj}, device_id_type=MESH).wait_recv()
            before_v[...] += shares[k] * tot_v[k]

    before = before_v[...]

    def carry_copy(k):
        return pltpu.make_async_remote_copy(
            src_ref=ca_out.at[k], dst_ref=ca_in.at[mj], send_sem=ca_send.at[k], recv_sem=ca_recv.at[mj],
            device_id=group_peer(k), device_id_type=MESH)

    def send_carry(k, carry):
        ca_out[k] = (pre_v[k] + fac_v[k] * before).astype(ca_out.dtype)

        @pl.when(k != mj)
        def _():
            carry_copy(k).start()

        return carry

    lax.fori_loop(0, nj, send_carry, 0)
    ca_in[mj] = ca_out[mj]

    lax.fori_loop(cut2, chunks, local_conv, 0)
    staged[6].wait()
    for copy in sq_copies:
        copy.wait_send()
    for d in range(1, ny):
        @pl.when(my + d < ny)
        def _():
            total_copy(d).wait_send()

    def drain_states(k, carry):
        @pl.when(k != mj)
        def _():
            state_copy(k).wait_send()

        return carry

    lax.fori_loop(0, nj, drain_states, 0)

    def await_block(b):

        @pl.when(b != mj)
        def _():
            pltpu.make_async_remote_copy(
                src_ref=ca_out.at[b], dst_ref=ca_in.at[b], send_sem=ca_send.at[b], recv_sem=ca_recv.at[b],
                device_id=group_peer(b), device_id_type=MESH).wait_recv()

    def finish(b):
        lanes = pl.ds(pl.multiple_of(b * LANES, LANES), LANES)
        jump = rows_of(jump_v[:, lanes])
        weight = ca_in[b].astype(F32)
        terms = [pow_v[b * modes + m] * weight[m:m + 1, :] for m in range(modes)]
        for t in range(tokens // 16):
            first = total_of(terms)
            terms = [a * c for a, c in zip(terms, jump)]
            second = total_of(terms)
            if t < tokens // 16 - 1:
                terms = [a * c for a, c in zip(terms, jump)]
            both = jnp.concatenate([first, second], axis=0) + conv_v[t * 16:(t + 1) * 16, lanes]
            gate = gate_v[t * 16:(t + 1) * 16, lanes].astype(F32)
            out_ref[t * 16:(t + 1) * 16, lanes] = (both * gate).astype(BF16)

    def finish_blocks(i, carry):
        pair = [lax.rem(mj + 2 * nj - spread(nj - 1 - 2 * i - n), nj) for n in range(2)]
        for b in pair:
            await_block(b)
        for b in pair:
            finish(b)
        return carry

    def drain_carries(k, carry):
        @pl.when(k != mj)
        def _():
            carry_copy(k).wait_send()

        return carry

    lax.fori_loop(0, blocks // 4, finish_blocks, 0)
    lax.fori_loop(0, nj, drain_carries, 0)
    lax.fori_loop(blocks // 4, blocks // 2, finish_blocks, 0)


def shards(nx, nseq, stream, norm_gain, gate_act, decay_rate, residue, skip_gain):
    tokens, chans = stream.shape
    modes = decay_rate.shape[1]
    blocks = chans // LANES
    nj = blocks
    ny = nseq // nj
    width = 256
    fwd, inv = half_tables(tokens)
    any_spec = pl.BlockSpec(memory_space=pl.ANY)
    vmem = pltpu.VMEM
    dma = pltpu.SemaphoreType.DMA
    return pl.pallas_call(
        functools.partial(kernel, nx, ny, nj, modes, width),
        out_shape=jax.ShapeDtypeStruct((tokens, chans), BF16),
        in_specs=[any_spec] * 8,
        out_specs=pl.BlockSpec(memory_space=pltpu.VMEM),
        scratch_shapes=[
            vmem((tokens, chans), BF16),
            vmem((tokens, chans), BF16),
            vmem((modes, chans), F32),
            vmem((modes, chans), F32),
            vmem((blocks, LANES), F32),
            vmem((blocks, LANES), F32),
            vmem(fwd.shape, BF16),
            vmem(inv.shape, BF16),
            vmem((tokens, LANES), F32),
            vmem((nx, 8, LANES), F32),
            vmem((tokens, LANES), F32),
            vmem((blocks * modes, 8, LANES), F32),
            vmem((tokens, chans), BF16),
            vmem((tokens, chans), F32),
            vmem((blocks * modes, 8, LANES), F32),
            vmem((modes, chans), F32),
            vmem((nj, modes, LANES), WIRE),
            vmem((nj, modes, LANES), WIRE),
            vmem((ny, modes, LANES), F32),
            vmem((modes, LANES), F32),
            vmem((nj, modes, LANES), F32),
            vmem((nj, modes, LANES), F32),
            vmem((nj, modes, LANES), WIRE),
            vmem((nj, modes, LANES), WIRE),
            dma((7,)),
            dma((4,)),
            dma((nx,)),
            dma((nx,)),
            dma((nj,)),
            dma((nj,)),
            dma((ny,)),
            dma((ny,)),
            dma((nj,)),
            dma((nj,)),
        ],
        compiler_params=pltpu.CompilerParams(
            collective_id=0, has_side_effects=True, vmem_limit_bytes=40 * 1024 * 1024
        ),
    )(*[pltpu.with_memory_space_constraint(v, pltpu.HBM) for v in (
        stream,
        decay_rate.T,
        residue.T,
        norm_gain.reshape(blocks, LANES),
        skip_gain.reshape(blocks, LANES),
        gate_act,
        jnp.asarray(fwd),
        jnp.asarray(inv),
    )])


def solution(mesh):
    in_specs = (P("seq", "ch"), P("ch"), P("seq", "ch"), P("ch", None), P("ch", None), P("ch"))
    body = functools.partial(shards, mesh.shape["ch"], mesh.shape["seq"])
    return jax.shard_map(body, mesh=mesh, in_specs=in_specs, out_specs=P("seq", "ch"), check_vma=False)
```
